512 devices in a mesh: sec: 2 (over core), dp: 64 (over z, y), mp: 4 (over x).
Axes of the slice: x: 4, y: 8, z: 8, core: 2. Of those that a mesh axis runs over, the one named last changes fastest.
Arguments:
- patches: bfloat16 [32768, 1280], P(('sec', 'dp'), 'mp'), may hold values from -6 to 6
- window_index: int32 [32768], P(('sec', 'dp')), may hold values from 0 to 3, as said below
- vit_gain: bfloat16 [1280], replicated, may hold values from 0.25 to 1.75
- vit_qkv: bfloat16 [1280, 3, 640], P(None, None, 'mp'), may hold values from -0.15625 to 0.15625
- vit_proj: bfloat16 [640, 1280], P('mp'), may hold values from -0.25 to 0.25
- merge_gain: bfloat16 [1280], replicated, may hold values from 0.25 to 1.75
- piece_rows: int32 [8192], P(('sec', 'dp')), may hold values from 0 to 2, as said below
- piece_dest: int32 [8192], P(('sec', 'dp')), may hold values from 0 to 127, as said below
- visual_kv: bfloat16 [5120, 2, 512], P('mp'), may hold values from -0.078125 to 0.078125
- text_query: bfloat16 [32768, 4096], P(('sec', 'dp'), 'mp'), may hold values from -8 to 8
- text_kv: bfloat16 [32768, 2, 512], P(('sec', 'dp'), None, 'mp'), may hold values from -8 to 8
- out_cotangent: bfloat16 [32768, 4096], P(('sec', 'dp'), 'mp'), may hold values from -6 to 6
Outputs:
- attended: bfloat16 [32768, 4096], P(('sec', 'dp'), 'mp')
- visual_grad: bfloat16 [8192, 5120], P(('sec', 'dp'), 'mp')
The draws below stay inside these ranges and needn't reach their ends.
Inputs may be any that keep to these rules, and one draw needn't show every extreme that they name: `window_index`: within each shard every window number names exactly 64 of its 256 patches. `piece_rows`: the 64 counts of a shard sum to 64; every shard has a piece of exactly 2 rows. `piece_dest`: the pieces of one shard go to distinct shards; in every draw some shard receives a piece of 2 rows from every shard.
All inputs are finite; a program needn't handle non-finite values.
Results may differ from the reference program's by a relative error of at most 0.02.
Values may be sent and summed in bfloat16 or wider, within the bound.
No kernel may reach another device: no remote copies, remote signals or barrier semaphores. Data moves between devices by JAX's collectives and lax.ppermute only.
A program may use at most 64 MiB of HBM per device.

```python
import math
import jax
import jax.numpy as jnp
from jax import lax

D_VIT = 1280
VIT_HEADS = 8
VIT_HD = 80
WIN = 64
MERGE = 4
PATCH_DEV = 256
Q_HEADS = 32
KV_HEADS = 4
HD = 128
TXT_DEV = 256
SHARDS = 128
M_DEV = 64
PIECES = 64
CAP = 2
SLOTS = 256
PATCHES = 32768
TEXT = 32768


def route_tables(key):
    hot = jax.random.randint(jax.random.fold_in(key, 11), (), 0, SHARDS)
    keys = jax.random.split(jax.random.fold_in(key, 12), SHARDS)

    def one_shard(shard_key):
        first_key, second_key = jax.random.split(shard_key)
        others = (hot + 1 + jax.random.permutation(first_key, SHARDS - 1)) % SHARDS
        dest = jnp.concatenate([hot[None], others[:PIECES - 1]]).astype(jnp.int32)
        leading = jax.random.randint(second_key, (PIECES // 2,), 0, CAP + 1)
        leading = leading.at[0].set(CAP)
        counts = jnp.stack([leading, CAP - leading], axis=1).reshape(PIECES)
        return (dest, counts.astype(jnp.int32))
    dest, counts = jax.vmap(one_shard)(keys)
    return (dest.reshape(-1), counts.reshape(-1))


def draw_piece_dest(key, part):
    return route_tables(key)[0]


def draw_piece_rows(key, part):
    return route_tables(key)[1]


def draw_window_index(key, part):
    key = jax.random.fold_in(key, 3)
    keys = jax.random.split(key, SHARDS)
    ids = jax.vmap(lambda shard_key: jax.random.permutation(shard_key, PATCH_DEV) // WIN)(keys)
    return ids.reshape(-1).astype(jnp.int32)


def draw_text_query(key, part):
    own_key = jax.random.fold_in(key, 5)
    shape = (SHARDS, TXT_DEV, KV_HEADS, Q_HEADS // KV_HEADS, HD)
    full = jnp.clip(jax.random.normal(own_key, shape, jnp.float32), -6.0, 6.0)
    return full.reshape(TEXT, Q_HEADS * HD).astype(jnp.bfloat16)


def draw_text_kv(key, part):
    own_key = jax.random.fold_in(key, 6)
    shape = (SHARDS, TXT_DEV, 2, KV_HEADS, HD)
    full = jnp.clip(jax.random.normal(own_key, shape, jnp.float32), -6.0, 6.0)
    return full.reshape(TEXT, 2, KV_HEADS * HD).astype(jnp.bfloat16)


def steps_of(stream_key, shape, pieces, smallest, top_value):
    level = 1.0
    for dim, shards_of in pieces:
        steps = jax.random.uniform(jax.random.fold_in(jax.random.fold_in(stream_key, 6), dim), (shards_of,), jnp.float32, smallest / len(pieces), top_value / len(pieces))
        level = level * jnp.repeat(jnp.exp(steps), shape[dim] // shards_of).reshape((-1,) + (1,) * (len(shape) - 1 - dim))
    return level


def gaussian(key, dims, deviation, bound, cuts=(), kind=jnp.bfloat16):
    array = jax.random.normal(key, dims, jnp.float32) * deviation
    if len(cuts) > 0:
        array = steps_of(key, dims, cuts, -0.22, 0.18) * array
    return jnp.clip(array, min=-bound, max=bound).astype(kind)


def setup_inputs(seed: int = 0) -> dict:
    splits = jax.random.split(jax.random.key(seed), 13)
    patches = gaussian(splits[0], (PATCHES, D_VIT), 1.0, 6.0, ((0, 128), (1, 4)))
    window_index = draw_window_index(jax.random.fold_in(splits[12], 71), 0)
    vit_gain = jnp.clip(1.0 + 0.15 * jax.random.normal(splits[2], (D_VIT,), jnp.float32), 0.25, 1.75).astype(jnp.bfloat16)
    vit_qkv = gaussian(splits[3], (D_VIT, 3, VIT_HEADS * VIT_HD), D_VIT ** -0.5, 0.15625, ((2, 4),))
    vit_proj = gaussian(splits[4], (VIT_HEADS * VIT_HD, D_VIT), (VIT_HEADS * VIT_HD) ** -0.5, 0.25, ((0, 4),))
    merge_gain = jnp.clip(1.0 + 0.15 * jax.random.normal(splits[5], (D_VIT,), jnp.float32), 0.25, 1.75).astype(jnp.bfloat16)
    piece_rows = draw_piece_rows(jax.random.fold_in(splits[12], 71), 0)
    piece_dest = draw_piece_dest(jax.random.fold_in(splits[12], 71), 0)
    visual_kv = gaussian(splits[8], (MERGE * D_VIT, 2, KV_HEADS * HD), (MERGE * D_VIT) ** -0.5, 0.078125, ((0, 4),))
    text_query = draw_text_query(jax.random.fold_in(splits[12], 71), 0)
    text_kv = draw_text_kv(jax.random.fold_in(splits[12], 71), 0)
    out_cotangent = gaussian(splits[11], (TEXT, Q_HEADS * HD), 1.0, 6.0, ((0, 128), (1, 4)))
    return {"patches": patches, "window_index": window_index, "vit_gain": vit_gain, "vit_qkv": vit_qkv, "vit_proj": vit_proj, "merge_gain": merge_gain, "piece_rows": piece_rows, "piece_dest": piece_dest, "visual_kv": visual_kv, "text_query": text_query, "text_kv": text_kv, "out_cotangent": out_cotangent}


def rms_scale(values, gain):
    mean = lax.optimization_barrier(jnp.mean(values * values, axis=-1, keepdims=True))
    return values * lax.rsqrt(mean + 1e-06) * gain

def attend(query, keys, values, allowed, cotangent):
    scale = 1.0 / math.sqrt(query.shape[-1])
    qf = query.astype(jnp.float32)
    kf = keys.astype(jnp.float32)
    vf = values.astype(jnp.float32)
    scores = jnp.einsum('ikgh,jkh->kgij', qf, kf) * scale
    scores = jnp.where(allowed[None, None], scores, -1e+30)
    top = lax.optimization_barrier(jnp.max(scores, axis=-1, keepdims=True))
    expo = jnp.exp(scores - top)
    probs = expo / lax.optimization_barrier(jnp.sum(expo, axis=-1, keepdims=True))
    weights = probs.astype(jnp.bfloat16)
    output = jnp.einsum('kgij,jkh->ikgh', weights.astype(jnp.float32), vf).astype(jnp.bfloat16)
    cf = cotangent.astype(jnp.float32)
    dprobs = jnp.einsum('ikgh,jkh->kgij', cf, vf)
    delta = lax.optimization_barrier(jnp.sum(probs * dprobs, axis=-1, keepdims=True))
    dscores = (probs * (dprobs - delta)).astype(jnp.bfloat16)
    dkeys = (jnp.einsum('kgij,ikgh->jkh', dscores.astype(jnp.float32), qf) * scale).astype(jnp.bfloat16)
    dvalues = jnp.einsum('kgij,ikgh->jkh', weights.astype(jnp.float32), cf).astype(jnp.bfloat16)
    return (output, dkeys, dvalues)

def vit_shard(inputs, vit_gain, vit_qkv, vit_proj, merge_gain):
    patch_rows, windows = inputs
    points = patch_rows.shape[0]
    width = vit_qkv.shape[2]
    normed = rms_scale(patch_rows.astype(jnp.float32), vit_gain.astype(jnp.float32)).astype(jnp.bfloat16)
    qkv = jnp.dot(normed, vit_qkv.reshape(D_VIT, 3 * width), preferred_element_type=jnp.float32).astype(jnp.bfloat16)
    qkv = qkv.reshape(points, 3, VIT_HEADS, VIT_HD).astype(jnp.float32)
    scores = jnp.einsum('phd,qhd->hpq', qkv[:, 0], qkv[:, 1]) / math.sqrt(VIT_HD)
    allowed = windows[:, None] == windows[None, :]
    scores = jnp.where(allowed[None], scores, -1e+30)
    top = lax.optimization_barrier(jnp.max(scores, axis=-1, keepdims=True))
    expo = jnp.exp(scores - top)
    weights = (expo / lax.optimization_barrier(jnp.sum(expo, axis=-1, keepdims=True))).astype(jnp.bfloat16)
    mixed = jnp.einsum('hpq,qhd->phd', weights.astype(jnp.float32), qkv[:, 2]).astype(jnp.bfloat16)
    update = jnp.dot(mixed.reshape(points, width), vit_proj, preferred_element_type=jnp.float32)
    resid = patch_rows.astype(jnp.float32) + update
    merged = rms_scale(resid, merge_gain.astype(jnp.float32)).astype(jnp.bfloat16)
    return merged.reshape(points // MERGE, MERGE * D_VIT)

def reference(patches, window_index, vit_gain, vit_qkv, vit_proj, merge_gain, piece_rows, piece_dest, visual_kv, text_query, text_kv, out_cotangent):
    shards = SHARDS
    group = Q_HEADS // KV_HEADS
    kv_width = KV_HEADS * HD
    inputs = (patches.reshape(shards, PATCH_DEV, D_VIT), window_index.reshape(shards, PATCH_DEV))
    merged = lax.map(lambda pair: vit_shard(pair, vit_gain, vit_qkv, vit_proj, merge_gain), inputs)
    kv_map = visual_kv.reshape(MERGE * D_VIT, 2 * kv_width)
    kv_rows = jnp.dot(merged.reshape(shards * M_DEV, MERGE * D_VIT), kv_map, preferred_element_type=jnp.float32)
    kv_rows = kv_rows.astype(jnp.bfloat16).reshape(shards, M_DEV, 2, KV_HEADS, HD)
    counts = piece_rows.reshape(shards, PIECES)
    dests = piece_dest.reshape(shards, PIECES)
    starts = jnp.cumsum(counts, axis=1) - counts
    offsets = jnp.arange(CAP, dtype=jnp.int32)
    sources = jnp.arange(shards, dtype=jnp.int32)[:, None]
    queries = text_query.reshape(shards, TXT_DEV, KV_HEADS, group, HD)
    cotangents = out_cotangent.reshape(shards, TXT_DEV, KV_HEADS, group, HD)
    text_pairs = text_kv.reshape(shards, TXT_DEV, 2, KV_HEADS, HD)
    causal = jnp.arange(TXT_DEV)[:, None] >= jnp.arange(TXT_DEV)[None, :]

    def per_dest(inputs_here):
        target, query, pairs, cotangent = inputs_here
        match = (dests == target).astype(jnp.int32)
        row_index = lax.optimization_barrier(jnp.sum(match[:, :, None] * (starts[:, :, None] + offsets[None, None, :]), axis=1))
        row_index = jnp.minimum(row_index, M_DEV - 1).astype(jnp.int32)
        inside = (offsets[None, None, :] < counts[:, :, None]).astype(jnp.int32)
        live = lax.optimization_barrier(jnp.sum(match[:, :, None] * inside, axis=1)) > 0
        gathered = kv_rows[sources, row_index].reshape(SLOTS, 2, KV_HEADS, HD)
        keys = jnp.concatenate([gathered[:, 0], pairs[:, 0]], axis=0)
        values = jnp.concatenate([gathered[:, 1], pairs[:, 1]], axis=0)
        allowed = jnp.concatenate([jnp.broadcast_to(live.reshape(1, SLOTS), (TXT_DEV, SLOTS)), causal], axis=1)
        output, dkeys, dvalues = attend(query, keys, values, allowed, cotangent)
        return (output.reshape(TXT_DEV, Q_HEADS * HD), jnp.stack([dkeys[:SLOTS], dvalues[:SLOTS]], axis=1))
    targets = jnp.arange(shards, dtype=jnp.int32)
    attended, slot_grads = lax.map(per_dest, (targets, queries, text_pairs, cotangents))
    rows = jnp.arange(M_DEV, dtype=jnp.int32)
    within = ((rows[None, None, :] >= starts[:, :, None]) & (rows[None, None, :] < (starts + counts)[:, :, None])).astype(jnp.int32)
    dest_row = lax.optimization_barrier(jnp.sum(within * dests[:, :, None], axis=1)).astype(jnp.int32)
    slot_row = (sources * CAP + lax.optimization_barrier(jnp.sum(within * (rows[None, None, :] - starts[:, :, None]), axis=1))).astype(jnp.int32)
    row_grads = slot_grads[dest_row, slot_row].reshape(shards * M_DEV, 2 * kv_width)
    visual_grad = jnp.dot(row_grads, kv_map.T, preferred_element_type=jnp.float32).astype(jnp.bfloat16)
    return (attended.reshape(TEXT, Q_HEADS * HD), visual_grad)
```

```python
import math

import jax
import jax.numpy as jnp
from jax import lax
from jax.experimental import pallas as pl
from jax.experimental.pallas import tpu as pltpu
from jax.sharding import PartitionSpec as P

VIT_HD = 80
HD = 128
EPS = 1e-6
NEG = -1e30
EMPTY = 2.0**100
LOG2E = math.log2(math.e)
F32 = jnp.float32
BF16 = jnp.bfloat16
VM = pl.BlockSpec(memory_space=pltpu.VMEM)
SM = pl.BlockSpec(memory_space=pltpu.SMEM)
TN = (((0,), (0,)), ((), ()))
NT = (((1,), (1,)), ((), ()))


def dot(a, b):
    return jnp.dot(a, b, preferred_element_type=F32)


def dotg(a, b, dims):
    return lax.dot_general(a, b, dims, preferred_element_type=F32)


def iota(shape, dim):
    return lax.broadcasted_iota(jnp.int32, shape, dim)


def call(kernel, out_shape, *args, flops=0, moved=0, limit=None, specs=None):
    return pl.pallas_call(
        kernel,
        out_shape=out_shape,
        in_specs=specs or [VM] * len(args),
        out_specs=jax.tree.map(lambda _: VM, out_shape),
        compiler_params=pltpu.CompilerParams(vmem_limit_bytes=limit or 16 * 2**20),
        cost_estimate=pl.CostEstimate(flops=flops, bytes_accessed=moved, transcendentals=0),
    )(*args)


def shape(dims, dtype=BF16):
    return jax.ShapeDtypeStruct(dims, dtype)


def prepare_kernel(
    wt_ref, gain_ref, win_ref, rows_ref, dest_ref, w_ref, bias_ref, pick_ref, pickt_ref, sent_ref
):
    w_ref[...] = (wt_ref[...].astype(F32) * gain_ref[...].astype(F32)).astype(BF16)
    wins = jnp.broadcast_to(win_ref[...].astype(F32), (256, 256))
    bias_ref[...] = jnp.where(wins == wins.T, 0.0, NEG)
    pieces = rows_ref.shape[1]
    a = iota((pieces, pieces), 0)
    b = iota((pieces, pieces), 1)
    rows = jnp.broadcast_to(rows_ref[...].astype(F32), (pieces, pieces))
    dest = jnp.broadcast_to(dest_ref[...].astype(F32), (pieces, pieces))
    starts = jnp.sum(jnp.where(b < a, rows, 0.0), axis=1, keepdims=True)
    count = jnp.sum(jnp.where(b == a, rows, 0.0), axis=1, keepdims=True)
    target = jnp.sum(jnp.where(b == a, dest, 0.0), axis=1, keepdims=True)
    lane = iota((pieces, 128), 1)
    row = (lane & 63).astype(F32)
    part = lane >> 6
    inside = (row >= starts) & (row < starts + count)
    code = jnp.sum(jnp.where(inside, target * 4.0 + row - starts, 0.0), axis=0, keepdims=True)
    code = code + 2.0 * part[:1].astype(F32)
    slots4 = pick_ref.shape[0]
    picks = jnp.where(iota((slots4, 128), 0).astype(F32) == code, 1.0, 0.0)
    pick_ref[...] = picks.astype(BF16)
    pickt_ref[...] = picks.T.astype(BF16)
    filled = jnp.sum(picks, axis=1, keepdims=True)
    key_row = (iota((slots4, 128), 0) & 2) == 0
    sent_ref[...] = jnp.where(key_row & (filled < 0.5), EMPTY, 0.0).astype(BF16)


def vit_kernel(pos_ref, x_ref, w_ref, bias_ref, proj_ref, part_ref, own_ref):
    x = x_ref[...]
    width, points = x.shape
    xf = x.astype(F32)
    scale = lax.rsqrt(jnp.sum(xf * xf, axis=0, keepdims=True) * (1.0 / width) + EPS)
    qkv = (dot(w_ref[...], x) * scale).astype(BF16)
    local = qkv.shape[0] // 3
    bias = bias_ref[...]
    mixed = []
    for h in range(local // VIT_HD):
        q = qkv[h * VIT_HD : (h + 1) * VIT_HD]
        k = qkv[local + h * VIT_HD : local + (h + 1) * VIT_HD]
        v = qkv[2 * local + h * VIT_HD : 2 * local + (h + 1) * VIT_HD]
        s = dotg(k, q, TN) * (LOG2E / math.sqrt(VIT_HD)) + bias
        e = jnp.exp2(s - jnp.max(s, axis=0, keepdims=True))
        weights = (e * (1.0 / jnp.sum(e, axis=0, keepdims=True))).astype(BF16)
        mixed.append(dot(v, weights).astype(BF16))
    mixed = jnp.concatenate(mixed, axis=0)
    n = iota((points, points), 1)
    perm = (iota((points, points), 0) == 4 * (n & 63) + (n >> 6)).astype(F32).astype(BF16)
    mixed = dot(mixed, perm).astype(BF16)
    part = dotg(mixed, proj_ref[...], TN).astype(BF16)
    for m in range(4):
        part_ref[m] = part[m * 64 : (m + 1) * 64]
    pos = pos_ref[0]
    sel = (iota((64, points), 1) == 4 * iota((64, points), 0) + pos).astype(F32).astype(BF16)
    own_ref[...] = dotg(sel, x, NT).astype(BF16)


def merge_kernel(in_ref, own_ref, gain_ref, w_ref, out_ref):
    resid = own_ref[...].astype(F32)
    for m in range(4):
        resid = resid + in_ref[m].astype(F32)
    scale = lax.rsqrt(jnp.mean(resid * resid, axis=1, keepdims=True) + EPS)
    merged = (resid * scale * gain_ref[...].astype(F32)).astype(BF16)
    kv = dot(merged, w_ref[...]).astype(BF16)
    for h in range(4):
        out_ref[h] = kv[:, h * 256 : (h + 1) * 256]


def pack_kernel(in_ref, pick_ref, sent_ref, out_ref):
    kv = in_ref[0].astype(F32)
    for m in range(1, 4):
        kv = kv + in_ref[m].astype(F32)
    kv = kv.astype(BF16)
    stack = jnp.concatenate([kv[:, :128], kv[:, 128:]], axis=0)
    out_ref[...] = (dot(pick_ref[...], stack) + sent_ref[...].astype(F32)).astype(BF16)


def text_kernel(
    q_ref, c_ref, k_ref, v_ref, qt_ref, ct_ref, ot_ref, m_ref, l_ref, d_ref, spread_ref, gather_ref
):
    rows = q_ref.shape[0]
    k = k_ref[...]
    v = v_ref[...]
    vt = v.T
    causal = iota((rows, rows), 0) <= iota((rows, rows), 1)
    for g in range(q_ref.shape[1] // HD):
        qt = q_ref[:, g * HD : (g + 1) * HD].T
        ct = c_ref[:, g * HD : (g + 1) * HD].T
        qt_ref[g] = qt
        ct_ref[g] = ct
        s = jnp.where(causal, dot(k, qt) * (LOG2E / math.sqrt(HD)), NEG)
        m = jnp.max(s, axis=0, keepdims=True)
        e = jnp.exp2(s - m)
        dp = dot(v, ct)
        m_ref[g : g + 1] = m
        l_ref[g : g + 1] = jnp.sum(e, axis=0, keepdims=True)
        d_ref[g : g + 1] = jnp.sum(e * dp, axis=0, keepdims=True)
        ot_ref[g] = dot(vt, e.astype(BF16))
    total = gather_ref.shape[0]
    half = total // 2
    a = iota((total, total), 0)
    b = iota((total, total), 1)

    def place(j):
        slot = j & (half - 1)
        return 4 * (slot >> 1) + 2 * (j >= half).astype(jnp.int32) + (slot & 1)

    gather_ref[...] = (b == place(a)).astype(F32).astype(BF16)
    spread_ref[...] = (a == place(b)).astype(F32).astype(BF16)


def slots_kernel(
    in_ref, gather_ref, spread_ref, q_ref, c_ref, qt_ref, ct_ref, m_ref, l_ref, d_ref,
    out_ref, w_ref, vt_ref, a_ref,
):
    slots = in_ref.shape[0] // 2
    kv = dot(gather_ref[...], in_ref[...])
    keys = kv[:slots]
    live = jnp.broadcast_to(keys[:, :1] < 0.5 * EMPTY, keys.shape)
    k = jnp.where(live, keys, 0.0).astype(BF16)
    v = kv[slots:].astype(BF16)
    vt_ref[...] = v.T
    bias = jnp.where(live, 0.0, NEG)
    bias = jnp.concatenate([bias, bias], axis=1)
    dk = jnp.zeros((slots, HD), F32)
    dv = jnp.zeros((slots, HD), F32)
    for g in range(qt_ref.shape[0]):
        s = dot(k, qt_ref[g]) * (LOG2E / math.sqrt(HD)) + bias
        dp = dot(v, ct_ref[g])
        mt = m_ref[g : g + 1]
        m = jnp.maximum(mt, jnp.max(s, axis=0, keepdims=True))
        e = jnp.exp2(s - m)
        alpha = jnp.exp2(mt - m)
        inv = 1.0 / (l_ref[g : g + 1] * alpha + jnp.sum(e, axis=0, keepdims=True))
        delta = (d_ref[g : g + 1] * alpha + jnp.sum(e * dp, axis=0, keepdims=True)) * inv
        a_ref[g : g + 1] = alpha * inv
        p = e * inv
        w = p.astype(BF16)
        ds = (p * (dp - delta)).astype(BF16)
        w_ref[g] = w
        dk = dk + dot(ds, q_ref[:, g * HD : (g + 1) * HD])
        dv = dv + dot(w, c_ref[:, g * HD : (g + 1) * HD])
    grads = jnp.concatenate([(dk * (1.0 / math.sqrt(HD))).astype(BF16), dv.astype(BF16)], axis=0)
    out_ref[...] = dot(spread_ref[...], grads).astype(BF16)


def output_kernel(ot_ref, a_ref, w_ref, vt_ref, out_ref):
    vt = vt_ref[...]
    for g in range(ot_ref.shape[0]):
        o = ot_ref[g] * a_ref[g : g + 1] + dot(vt, w_ref[g])
        out_ref[:, g * HD : (g + 1) * HD] = o.T.astype(BF16)


def rows_kernel(in_ref, pickt_ref, out_ref):
    g = dot(pickt_ref[...], in_ref[...]).astype(BF16)
    half = g.shape[0] // 2
    for m in range(4):
        out_ref[m, :, :HD] = g[:half]
        out_ref[m, :, HD:] = g[half:]


def fold_kernel(in_ref, w_ref, out_ref):
    grads = jnp.concatenate([in_ref[h] for h in range(4)], axis=1)
    out_ref[...] = dotg(grads, w_ref[...], NT).astype(BF16)


def exchange(x, axes):
    return lax.all_to_all(x, axes, split_axis=0, concat_axis=0, tiled=True)


def on_device(
    patches, window_index, vit_gain, vit_qkv, vit_proj, merge_gain, piece_rows, piece_dest,
    visual_kv, text_query, text_kv, out_cotangent,
):
    shards = lax.axis_size("sec") * lax.axis_size("dp")
    position = lax.axis_index("mp").astype(jnp.int32).reshape(1)
    points, width_part = patches.shape
    width = vit_qkv.shape[0]
    local = vit_qkv.shape[2]
    rows = text_query.shape[0]
    slots = 2 * shards
    merged_rows = points // 4

    gathered = exchange(jnp.broadcast_to(patches.T[None], (4, width_part, points)), "mp")
    x = gathered.reshape(width, points)
    wt = jnp.transpose(vit_qkv, (1, 2, 0)).reshape(3 * local, width)
    w_qkv, bias, pick, pickt, sent = call(
        prepare_kernel,
        (
            shape((3 * local, width)),
            shape((points, points), F32),
            shape((2 * slots, 128)),
            shape((128, 2 * slots)),
            shape((2 * slots, 128)),
        ),
        wt, vit_gain.reshape(1, width), window_index.reshape(1, points),
        piece_rows.reshape(1, -1), piece_dest.reshape(1, -1),
        flops=10**8, moved=3 * 10**6,
    )
    part, own = call(
        vit_kernel,
        (shape((4, merged_rows, width)), shape((merged_rows, width))),
        position, x, w_qkv, bias, vit_proj,
        specs=[SM] + [VM] * 4, flops=10**9, moved=4 * 10**6, limit=32 * 2**20,
    )
    summed = exchange(part, "mp")
    w_kv = jnp.transpose(visual_kv.reshape(width, 2, 4, HD), (0, 2, 1, 3)).reshape(width, 8 * HD)
    kv_part = call(
        merge_kernel, shape((4, merged_rows, 2 * HD)),
        summed, own, merge_gain.reshape(1, width), w_kv, flops=2 * 10**8, moved=4 * 10**6,
    )
    kv_terms = exchange(kv_part, "mp")
    outgoing = call(
        pack_kernel, shape((2 * slots, HD)), kv_terms, pick, sent, flops=2 * 10**7, moved=10**6,
    )
    incoming = exchange(outgoing.reshape(shards, 4, HD), ("sec", "dp")).reshape(2 * slots, HD)

    group = text_query.shape[1] // HD
    qt, ct, ot, top, total, delta, spread, gather = call(
        text_kernel,
        (
            shape((group, HD, rows)), shape((group, HD, rows)), shape((group, HD, rows), F32),
            shape((group, rows), F32), shape((group, rows), F32), shape((group, rows), F32),
            shape((2 * slots, 2 * slots)), shape((2 * slots, 2 * slots)),
        ),
        text_query, out_cotangent, text_kv[:, 0], text_kv[:, 1],
        flops=2 * 10**9, moved=5 * 10**6, limit=32 * 2**20,
    )
    grads, weights, vt, ratio = call(
        slots_kernel,
        (
            shape((2 * slots, HD)), shape((group, slots, rows)), shape((HD, slots)),
            shape((group, rows), F32),
        ),
        incoming, gather, spread, text_query, out_cotangent, qt, ct, top, total, delta,
        flops=2 * 10**9, moved=5 * 10**6, limit=32 * 2**20,
    )
    returned = exchange(grads.reshape(shards, 4, HD), ("sec", "dp")).reshape(2 * slots, HD)
    attended = call(
        output_kernel, shape((rows, group * HD)), ot, ratio, weights, vt,
        flops=2 * 10**9, moved=3 * 10**6, limit=32 * 2**20,
    )
    row_grads = call(
        rows_kernel, shape((4, merged_rows, 2 * HD)), returned, pickt, flops=2 * 10**7, moved=5 * 10**5,
    )
    heads = exchange(row_grads, "mp")
    visual_grad = call(
        fold_kernel, shape((merged_rows, width)), heads, w_kv, flops=2 * 10**8, moved=3 * 10**6,
    )
    return (attended, visual_grad)


def solution(mesh):
    both = ("sec", "dp")
    in_specs = (
        P(both, "mp"), P(both), P(), P(None, None, "mp"), P("mp", None), P(), P(both), P(both),
        P("mp", None, None), P(both, "mp"), P(both, None, "mp"), P(both, "mp"),
    )
    return jax.shard_map(
        on_device, mesh=mesh, in_specs=in_specs, out_specs=(P(both, "mp"), P(both, "mp")),
        check_vma=False,
    )
```

```python
import math

import jax
import jax.numpy as jnp
from jax import lax
from jax.experimental import pallas as pl
from jax.experimental.pallas import tpu as pltpu
from jax.sharding import PartitionSpec as P

VIT_HD = 80
HD = 128
EPS = 1e-6
NEG = -1e30
EMPTY = 2.0**100
WIDE = 59
LOG2E = math.log2(math.e)
SCALE2 = LOG2E / math.sqrt(HD)
F32 = jnp.float32
BF16 = jnp.bfloat16
VM = pl.BlockSpec(memory_space=pltpu.VMEM)
SM = pl.BlockSpec(memory_space=pltpu.SMEM)
ANY = pl.BlockSpec(memory_space=pl.ANY)
DMA = pltpu.SemaphoreType.DMA


def dot(a, b):
    return jnp.dot(a, b, preferred_element_type=F32)


def iota(shape, dim):
    return lax.broadcasted_iota(jnp.int32, shape, dim)


def call(kernel, out_shape, *args, flops=0, moved=0, limit=6, specs=None, out_specs=None, scratch=()):
    return pl.pallas_call(
        kernel,
        out_shape=out_shape,
        in_specs=specs or [VM] * len(args),
        out_specs=out_specs or jax.tree.map(lambda _: VM, out_shape),
        scratch_shapes=scratch,
        compiler_params=limit and pltpu.CompilerParams(vmem_limit_bytes=limit * 2**20),
        cost_estimate=pl.CostEstimate(flops=flops, bytes_accessed=moved, transcendentals=0),
    )(*args)


def shape(dims, dtype=BF16):
    return jax.ShapeDtypeStruct(dims, dtype)


def one_hot(mask):
    return mask.astype(F32).astype(BF16)


def fetch(pairs, sems):
    copies = [pltpu.make_async_copy(a, b, sems.at[i]) for i, (a, b) in enumerate(pairs)]
    for copy in copies:
        copy.start()
    return copies


def code_kernel(rows_ref, dest_ref, code_ref):
    pieces = rows_ref.shape[1]
    a = iota((pieces, pieces), 0)
    b = iota((pieces, pieces), 1)
    rows = jnp.broadcast_to(rows_ref[...].astype(F32), (pieces, pieces))
    dest = jnp.broadcast_to(dest_ref[...].astype(F32), (pieces, pieces))
    starts = jnp.sum(jnp.where(b < a, rows, 0.0), axis=1, keepdims=True)
    count = jnp.sum(jnp.where(b == a, rows, 0.0), axis=1, keepdims=True)
    target = jnp.sum(jnp.where(b == a, dest, 0.0), axis=1, keepdims=True)
    lane = iota((pieces, HD), 1)
    row = (lane & 63).astype(F32)
    inside = (row >= starts) & (row < starts + count)
    code = jnp.sum(jnp.where(inside, target * 4.0 + row - starts, 0.0), axis=0, keepdims=True)
    code_ref[...] = jnp.broadcast_to(code, (8, HD)) + 2.0 * (iota((8, HD), 1) >> 6).astype(F32)


def vit_kernel(
    pos_ref, gain_hbm, win_hbm, wt_hbm, x_hbm, proj_hbm, part_ref, own_ref,
    gain_ref, win_ref, wt_ref, x_ref, proj_ref, w_ref, sems,
):
    pairs = [(gain_hbm, gain_ref), (x_hbm, x_ref), (wt_hbm, wt_ref)]
    pairs += [(win_hbm, win_ref), (proj_hbm, proj_ref)]
    copies = fetch(pairs, sems)
    width, points = x_ref.shape
    copies[0].wait()
    copies[1].wait()
    x = x_ref[...]
    local = proj_ref.shape[0]
    xf = x.astype(F32)
    scale = lax.rsqrt(jnp.sum(xf * xf, axis=0, keepdims=True) * (1.0 / width) + EPS)
    copies[2].wait()
    for i in range(width // HD):
        cols = slice(i * HD, (i + 1) * HD)
        w_ref[:, cols] = (wt_ref[:, cols].astype(F32) * gain_ref[i : i + 1].astype(F32)).astype(BF16)
    qkv = (dot(w_ref[...], x) * scale).astype(BF16)
    copies[3].wait()
    wins = jnp.broadcast_to(win_ref[...].astype(F32), (8, points))
    bias = jnp.where(wins.T[:, :1] == wins[:1], 0.0, NEG)
    mixed = []
    for h in range(local // VIT_HD):
        q = qkv[h * VIT_HD : (h + 1) * VIT_HD]
        k = qkv[local + h * VIT_HD : local + (h + 1) * VIT_HD]
        v = qkv[2 * local + h * VIT_HD : 2 * local + (h + 1) * VIT_HD]
        s = dot(k.T, q) * (LOG2E / math.sqrt(VIT_HD)) + bias
        e = jnp.exp2(s - jnp.max(s, axis=0, keepdims=True))
        weights = (e * (1.0 / jnp.sum(e, axis=0, keepdims=True))).astype(BF16)
        mixed.append(dot(v, weights).astype(BF16))
    mixed = jnp.concatenate(mixed, axis=0)
    n = iota((points, points), 1)
    perm = one_hot(iota((points, points), 0) == 4 * (n & 63) + (n >> 6))
    mixed = dot(mixed, perm).astype(BF16)
    copies[4].wait()
    part = dot(mixed.T, proj_ref[...]).astype(BF16)
    for m in range(4):
        part_ref[m] = part[m * 64 : (m + 1) * 64]
    sel = one_hot(iota((points, 64), 0) == 4 * iota((points, 64), 1) + pos_ref[0])
    own_ref[...] = dot(x, sel).astype(BF16).T


def merge_kernel(in_ref, own_ref, gain_ref, w_ref, out_ref):
    resid = own_ref[...].astype(F32)
    for m in range(4):
        resid = resid + in_ref[m].astype(F32)
    scale = lax.rsqrt(jnp.mean(resid * resid, axis=1, keepdims=True) + EPS)
    merged = (resid * scale * gain_ref[...].astype(F32)).astype(BF16)
    kv = dot(merged, w_ref[...]).astype(BF16)
    for h in range(4):
        out_ref[h] = kv[:, h * 256 : (h + 1) * 256]


def pack_kernel(in_ref, code_hbm, out_ref, code_ref, sems):
    copies = fetch([(code_hbm, code_ref)], sems)
    kv = in_ref[0].astype(F32)
    for m in range(1, 4):
        kv = kv + in_ref[m].astype(F32)
    kv = kv.astype(BF16)
    stack = jnp.concatenate([kv[:, :HD], kv[:, HD:]], axis=0)
    copies[0].wait()
    dims = out_ref.shape
    row = iota(dims, 0)
    picks = one_hot(row.astype(F32) == code_ref[:1])
    filled = dot(picks, jnp.ones((HD, HD), BF16))
    empty = jnp.where(((row & 2) == 0) & (filled < 0.5), EMPTY, 0.0)
    out_ref[...] = (dot(picks, stack) + empty).astype(BF16)


def halves(ref):
    half = ref.shape[1] // 2
    return [ref.at[:, :half], ref.at[:, half:]]


def fetch_wide(q_hbm, c_hbm, q_ref, c_ref, sems):
    pairs = list(zip(halves(q_hbm) + halves(c_hbm), halves(q_ref) + halves(c_ref)))
    q0, q1, c0, c1 = pairs
    return fetch([q0, c0, q1, c1], sems)


def text_kernel(kv_hbm, q_hbm, c_hbm, stats_ref, kv_ref, q_ref, c_ref, sems):
    head = fetch([(kv_hbm, kv_ref)], sems.at[pl.ds(0, 1)])[0]
    copies = fetch_wide(q_hbm, c_hbm, q_ref, c_ref, sems.at[pl.ds(1, 4)])
    group = q_ref.shape[1] // HD
    rows = q_ref.shape[0]
    head.wait()
    k, v = text_pair(kv_ref)
    causal = iota((rows, rows), 0) <= iota((rows, rows), 1)
    for g in range(group):
        if g % (group // 2) == 0:
            for copy in copies[:2] if g == 0 else copies[2:]:
                copy.wait()
        s = jnp.where(causal, dot(k, q_ref[:, g * HD : (g + 1) * HD].T) * SCALE2, NEG)
        m = jnp.max(s, axis=0, keepdims=True)
        e = jnp.exp2(s - m)
        dp = dot(v, c_ref[:, g * HD : (g + 1) * HD].T)
        stats_ref[g : g + 1] = m
        stats_ref[group + g : group + g + 1] = jnp.sum(e, axis=0, keepdims=True)
        stats_ref[2 * group + g : 2 * group + g + 1] = jnp.sum(e * dp, axis=0, keepdims=True)


def text_pair(kv_ref):
    a = iota((HD, HD), 0)
    order = one_hot(iota((HD, HD), 1) == 2 * (a & 63) + (a >> 6))
    return split(order, kv_ref)


def split(order, ref):
    keys = []
    values = []
    for b in range(ref.shape[0] // HD):
        part = dot(order, ref[b * HD : (b + 1) * HD]).astype(BF16)
        keys.append(part[:64])
        values.append(part[64:])
    return jnp.concatenate(keys, axis=0), jnp.concatenate(values, axis=0)


def slot_place(j):
    return 4 * ((j & 63) >> 1) + 2 * (j >> 6) + (j & 1)


def slot_pair(in_ref):
    order = one_hot(iota((HD, HD), 1) == slot_place(iota((HD, HD), 0)))
    keys, values = split(order, in_ref)
    live = jnp.broadcast_to(keys[:, :1].astype(F32) < 0.5 * EMPTY, keys.shape)
    bias = jnp.where(live, 0.0, NEG)
    keys = jnp.where(live, keys.astype(F32), 0.0).astype(BF16)
    return keys, values, jnp.concatenate([bias, bias], axis=1)


def slots_kernel(
    in_hbm, text_hbm, q_hbm, c_hbm, out_ref, stats_ref, in_ref, text_ref, q_ref, c_ref, sems
):
    head, stats = fetch([(in_hbm, in_ref), (text_hbm, text_ref)], sems.at[pl.ds(0, 2)])
    copies = fetch_wide(q_hbm, c_hbm, q_ref, c_ref, sems.at[pl.ds(2, 4)])
    group = q_ref.shape[1] // HD
    head.wait()
    k, v, bias = slot_pair(in_ref)
    slots = k.shape[0]
    stats.wait()
    dk = jnp.zeros((slots, HD), F32)
    dv = jnp.zeros((slots, HD), F32)
    for g in range(group):
        if g % (group // 2) == 0:
            for copy in copies[:2] if g == 0 else copies[2:]:
                copy.wait()
        q = q_ref[:, g * HD : (g + 1) * HD]
        c = c_ref[:, g * HD : (g + 1) * HD]
        s = dot(k, q.T) * SCALE2 + bias
        dp = dot(v, c.T)
        mt = text_ref[g : g + 1]
        m = jnp.maximum(mt, jnp.max(s, axis=0, keepdims=True))
        e = jnp.exp2(s - m)
        alpha = jnp.exp2(mt - m)
        total = text_ref[group + g : group + g + 1] * alpha + jnp.sum(e, axis=0, keepdims=True)
        inv = 1.0 / total
        delta = text_ref[2 * group + g : 2 * group + g + 1] * alpha
        delta = (delta + jnp.sum(e * dp, axis=0, keepdims=True)) * inv
        stats_ref[g : g + 1] = m
        stats_ref[group + g : group + g + 1] = inv
        p = e * inv
        ds = (p * (dp - delta)).astype(BF16)
        dk = dk + dot(ds, q)
        dv = dv + dot(p.astype(BF16), c)
    dk = (dk * (1.0 / math.sqrt(HD))).astype(BF16)
    dv = dv.astype(BF16)
    order = one_hot(iota((HD, HD), 0) == slot_place(iota((HD, HD), 1)))
    for b in range(slots // 64):
        pair = jnp.concatenate([dk[b * 64 : (b + 1) * 64], dv[b * 64 : (b + 1) * 64]], axis=0)
        out_ref[b * HD : (b + 1) * HD] = dot(order, pair).astype(BF16)


def output_kernel(
    in_hbm, kv_hbm, stats_hbm, q_hbm, out_ref, in_ref, kv_ref, stats_ref, q_ref, sems
):
    pairs = [(in_hbm, in_ref), (kv_hbm, kv_ref), (stats_hbm, stats_ref), (q_hbm, q_ref)]
    for copy in fetch(pairs, sems):
        copy.wait()
    group = q_ref.shape[1] // HD
    rows = q_ref.shape[0]
    kt, vt = text_pair(kv_ref)
    ks, vs, bias = slot_pair(in_ref)
    vt = vt.T
    vs = vs.T
    causal = iota((rows, rows), 0) <= iota((rows, rows), 1)
    for g in range(group):
        qt = q_ref[:, g * HD : (g + 1) * HD].T
        m = stats_ref[g : g + 1]
        inv = stats_ref[group + g : group + g + 1]
        s = jnp.where(causal, dot(kt, qt) * SCALE2, NEG)
        o = dot(vt, (jnp.exp2(s - m) * inv).astype(BF16))
        s = dot(ks, qt) * SCALE2 + bias
        o = o + dot(vs, (jnp.exp2(s - m) * inv).astype(BF16))
        out_ref[:, g * HD : (g + 1) * HD] = o.T.astype(BF16)


def rows_kernel(in_ref, code_ref, out_ref):
    code = jnp.broadcast_to(code_ref[:1], (HD, HD)).T
    count = in_ref.shape[0]
    picks = one_hot(iota((HD, count), 1).astype(F32) == code[:, :1])
    g = dot(picks, in_ref[...]).astype(BF16)
    half = HD // 2
    for m in range(4):
        out_ref[m, :, :HD] = g[:half]
        out_ref[m, :, HD:] = g[half:]


def fold_kernel(in_ref, w_ref, out_ref):
    grads = jnp.concatenate([in_ref[h] for h in range(4)], axis=1)
    out_ref[...] = dot(w_ref[...], grads.T).T.astype(BF16)


def exchange(x, axes):
    return lax.all_to_all(x, axes, split_axis=0, concat_axis=0, tiled=True)


def on_device(
    patches, window_index, vit_gain, vit_qkv, vit_proj, merge_gain, piece_rows, piece_dest,
    visual_kv, text_query, text_kv, out_cotangent,
):
    shards = lax.axis_size("sec") * lax.axis_size("dp")
    position = lax.axis_index("mp").astype(jnp.int32).reshape(1)
    points, width_part = patches.shape
    width = vit_qkv.shape[0]
    local = vit_qkv.shape[2]
    rows = text_query.shape[0]
    slots = 2 * shards
    merged_rows = points // 4

    x = lax.all_gather(patches.T, "mp", axis=0, tiled=True)
    wt = jnp.transpose(vit_qkv, (1, 2, 0)).reshape(3 * local, width)
    part, own = call(
        vit_kernel, (shape((4, merged_rows, width)), shape((merged_rows, width))),
        position, vit_gain.reshape(-1, HD), window_index.reshape(1, points), wt, x, vit_proj,
        specs=[SM] + [ANY] * 5, limit=WIDE, flops=10**9, moved=4 * 10**6,
        scratch=[
            pltpu.VMEM((width // HD, HD), BF16), pltpu.VMEM((1, points), jnp.int32),
            pltpu.VMEM((3 * local, width), BF16), pltpu.VMEM((width, points), BF16),
            pltpu.VMEM((local, width), BF16), pltpu.VMEM((3 * local, width), BF16), DMA((5,)),
        ],
    )
    code = call(
        code_kernel, shape((8, HD), F32), piece_rows.reshape(1, -1), piece_dest.reshape(1, -1),
        flops=10**6, moved=10**4,
    )
    summed = exchange(part, "mp")
    w_kv = jnp.transpose(visual_kv.reshape(width, 2, 4, HD), (0, 2, 1, 3)).reshape(width, 8 * HD)
    kv_part = call(
        merge_kernel, shape((4, merged_rows, 2 * HD)),
        summed, own, merge_gain.reshape(1, width), w_kv, flops=2 * 10**8, moved=4 * 10**6,
    )
    kv_terms = exchange(kv_part, "mp")
    group = text_query.shape[1] // HD
    text_rows = text_kv.reshape(2 * rows, HD)
    wide = pltpu.VMEM((rows, group * HD), BF16)
    thin = pltpu.VMEM((2 * rows, HD), BF16)
    stats = call(
        text_kernel, shape((3 * group, rows), F32), text_rows, text_query, out_cotangent,
        specs=[ANY] * 3, scratch=[thin, wide, wide, DMA((5,))], limit=WIDE,
        flops=10**9, moved=2 * 10**6,
    )
    kv_terms, stats = lax.optimization_barrier((kv_terms, stats))
    outgoing = call(
        pack_kernel, shape((2 * slots, HD)), kv_terms, code, specs=[VM, ANY],
        scratch=[pltpu.VMEM((8, HD), F32), DMA((1,))], flops=2 * 10**7, moved=10**6,
    )
    route = ("sec", "dp")
    incoming = exchange(outgoing.reshape(shards, 4, HD), route).reshape(2 * slots, HD)
    slot_rows = pltpu.VMEM(incoming.shape, BF16)
    grads, stats = call(
        slots_kernel, (shape((2 * slots, HD)), shape((2 * group, rows), F32)),
        incoming, stats, text_query, out_cotangent, specs=[ANY] * 4, limit=WIDE,
        scratch=[slot_rows, pltpu.VMEM(stats.shape, F32), wide, wide, DMA((6,))],
        flops=10**9, moved=2 * 10**6,
    )
    returned = exchange(grads.reshape(shards, 4, HD), route).reshape(2 * slots, HD)
    attended = call(
        output_kernel, shape((rows, group * HD)), incoming, text_rows, stats, text_query,
        specs=[ANY] * 4, scratch=[slot_rows, thin, pltpu.VMEM(stats.shape, F32), wide, DMA((4,))],
        limit=WIDE, flops=10**9, moved=2 * 10**6,
    )
    returned, attended = lax.optimization_barrier((returned, attended))
    row_grads = call(
        rows_kernel, shape((4, merged_rows, 2 * HD)), returned, code, flops=2 * 10**7, moved=5 * 10**5,
    )
    heads = exchange(row_grads, "mp")
    visual_grad = call(
        fold_kernel, shape((merged_rows, width)), heads, w_kv, flops=2 * 10**8, moved=3 * 10**6,
    )
    return (attended, visual_grad)


def solution(mesh):
    both = ("sec", "dp")
    in_specs = (
        P(both, "mp"), P(both), P(), P(None, None, "mp"), P("mp", None), P(), P(both), P(both),
        P("mp", None, None), P(both, "mp"), P(both, None, "mp"), P(both, "mp"),
    )
    return jax.shard_map(
        on_device, mesh=mesh, in_specs=in_specs, out_specs=(P(both, "mp"), P(both, "mp")),
        check_vma=False,
    )
```

```python
import math

import jax
import jax.numpy as jnp
from jax import lax
from jax.experimental import pallas as pl
from jax.experimental.pallas import tpu as pltpu
from jax.sharding import PartitionSpec as P

VIT_HD = 80
HD = 128
EPS = 1e-6
NEG = -1e30
EMPTY = 2.0**100
WIDE = 59
DP = 64
SLOTL = 53.5
LOG2E = math.log2(math.e)
SCALE2 = LOG2E / math.sqrt(HD)
F32 = jnp.float32
BF16 = jnp.bfloat16
VM = pl.BlockSpec(memory_space=pltpu.VMEM)
SM = pl.BlockSpec(memory_space=pltpu.SMEM)
ANY = pl.BlockSpec(memory_space=pl.ANY)
DMA = pltpu.SemaphoreType.DMA


def dot(a, b):
    return jnp.dot(a, b, preferred_element_type=F32)


def iota(shape, dim):
    return lax.broadcasted_iota(jnp.int32, shape, dim)


def call(kernel, out_shape, *args, flops=0, moved=0, limit=6, specs=None, out_specs=None, scratch=()):
    return pl.pallas_call(
        kernel,
        out_shape=out_shape,
        in_specs=specs or [VM] * len(args),
        out_specs=out_specs or jax.tree.map(lambda _: VM, out_shape),
        scratch_shapes=scratch,
        compiler_params=limit and pltpu.CompilerParams(vmem_limit_bytes=int(limit * 2**20)),
        cost_estimate=pl.CostEstimate(flops=flops, bytes_accessed=moved, transcendentals=0),
    )(*args)


def shape(dims, dtype=BF16):
    return jax.ShapeDtypeStruct(dims, dtype)


def one_hot(mask):
    return mask.astype(F32).astype(BF16)


def fetch(pairs, sems):
    copies = [pltpu.make_async_copy(a, b, sems.at[i]) for i, (a, b) in enumerate(pairs)]
    for copy in copies:
        copy.start()
    return copies


def code_kernel(rows_ref, dest_ref, code_ref):
    pieces = rows_ref.shape[1]
    a = iota((pieces, pieces), 0)
    b = iota((pieces, pieces), 1)
    rows = jnp.broadcast_to(rows_ref[...].astype(F32), (pieces, pieces))
    place = dest_ref[...]
    place = (place & (DP - 1)) * 2 + (place >> (DP.bit_length() - 1))
    dest = jnp.broadcast_to(place.astype(F32), (pieces, pieces))
    starts = jnp.sum(jnp.where(b < a, rows, 0.0), axis=1, keepdims=True)
    count = jnp.sum(jnp.where(b == a, rows, 0.0), axis=1, keepdims=True)
    target = jnp.sum(jnp.where(b == a, dest, 0.0), axis=1, keepdims=True)
    lane = iota((pieces, HD), 1)
    row = (lane & 63).astype(F32)
    inside = (row >= starts) & (row < starts + count)
    code = jnp.sum(jnp.where(inside, target * 4.0 + row - starts, 0.0), axis=0, keepdims=True)
    code_ref[...] = jnp.broadcast_to(code, (8, HD)) + 2.0 * (iota((8, HD), 1) >> 6).astype(F32)


def vit_kernel(
    pos_ref, gain_hbm, win_hbm, wt_hbm, x_hbm, proj_hbm, part_ref, own_ref,
    gain_ref, win_ref, wt_ref, x_ref, proj_ref, w_ref, sems,
):
    pairs = [(gain_hbm, gain_ref), (x_hbm, x_ref), (wt_hbm, wt_ref)]
    pairs += [(win_hbm, win_ref), (proj_hbm, proj_ref)]
    copies = fetch(pairs, sems)
    width, points = x_ref.shape
    copies[0].wait()
    copies[1].wait()
    x = x_ref[...]
    local = proj_ref.shape[0]
    xf = x.astype(F32)
    scale = lax.rsqrt(jnp.sum(xf * xf, axis=0, keepdims=True) * (1.0 / width) + EPS)
    copies[2].wait()
    for i in range(width // HD):
        cols = slice(i * HD, (i + 1) * HD)
        w_ref[:, cols] = (wt_ref[:, cols].astype(F32) * gain_ref[i : i + 1].astype(F32)).astype(BF16)
    qkv = (dot(w_ref[...], x) * scale).astype(BF16)
    copies[3].wait()
    wins = jnp.broadcast_to(win_ref[...].astype(F32), (8, points))
    bias = jnp.where(wins.T[:, :1] == wins[:1], 0.0, NEG)
    mixed = []
    for h in range(local // VIT_HD):
        q = qkv[h * VIT_HD : (h + 1) * VIT_HD]
        k = qkv[local + h * VIT_HD : local + (h + 1) * VIT_HD]
        v = qkv[2 * local + h * VIT_HD : 2 * local + (h + 1) * VIT_HD]
        s = dot(k.T, q) * (LOG2E / math.sqrt(VIT_HD)) + bias
        e = jnp.exp2(s - jnp.max(s, axis=0, keepdims=True))
        weights = (e * (1.0 / jnp.sum(e, axis=0, keepdims=True))).astype(BF16)
        mixed.append(dot(v, weights).astype(BF16))
    mixed = jnp.concatenate(mixed, axis=0)
    n = iota((points, points), 1)
    perm = one_hot(iota((points, points), 0) == 4 * (n & 63) + (n >> 6))
    mixed = dot(mixed, perm).astype(BF16)
    copies[4].wait()
    part = dot(mixed.T, proj_ref[...]).astype(BF16)
    for m in range(4):
        part_ref[m] = part[m * 64 : (m + 1) * 64]
    sel = one_hot(iota((points, 64), 0) == 4 * iota((points, 64), 1) + pos_ref[0])
    own_ref[...] = dot(x, sel).astype(BF16).T


def merge_kernel(in_ref, own_ref, gain_ref, w_ref, out_ref):
    resid = own_ref[...].astype(F32)
    for m in range(4):
        resid = resid + in_ref[m].astype(F32)
    scale = lax.rsqrt(jnp.mean(resid * resid, axis=1, keepdims=True) + EPS)
    merged = (resid * scale * gain_ref[...].astype(F32)).astype(BF16)
    kv = dot(merged, w_ref[...]).astype(BF16)
    for h in range(4):
        out_ref[h] = kv[:, h * 256 : (h + 1) * 256]


def pack_kernel(in_ref, code_hbm, out_ref, code_ref, sems):
    copies = fetch([(code_hbm, code_ref)], sems)
    kv = in_ref[0].astype(F32)
    for m in range(1, 4):
        kv = kv + in_ref[m].astype(F32)
    kv = kv.astype(BF16)
    stack = jnp.concatenate([kv[:, :HD], kv[:, HD:]], axis=0)
    copies[0].wait()
    dims = out_ref.shape
    row = iota(dims, 0)
    picks = one_hot(row.astype(F32) == code_ref[:1])
    filled = dot(picks, jnp.ones((HD, HD), BF16))
    empty = jnp.where(((row & 2) == 0) & (filled < 0.5), EMPTY, 0.0)
    out_ref[...] = (dot(picks, stack) + empty).astype(BF16)


def head_of(tall, ref):
    return tall.at[pl.ds(0, ref.shape[0])]


def halves(ref):
    half = ref.shape[1] // 2
    return [ref.at[:, :half], ref.at[:, half:]]


def fetch_wide(q_hbm, c_hbm, q_ref, c_ref, sems):
    pairs = list(zip(halves(q_hbm) + halves(c_hbm), halves(q_ref) + halves(c_ref)))
    q0, q1, c0, c1 = pairs
    return fetch([q0, c0, q1, c1], sems)


def text_kernel(kv_hbm, q_hbm, c_hbm, stats_hbm, kv_ref, q_ref, c_ref, stats_ref, sems):
    head = fetch([(kv_hbm, kv_ref)], sems.at[pl.ds(0, 1)])[0]
    copies = fetch_wide(q_hbm, c_hbm, q_ref, c_ref, sems.at[pl.ds(1, 4)])
    group = q_ref.shape[1] // HD
    rows = q_ref.shape[0]
    head.wait()
    k, v = text_pair(kv_ref)
    causal = iota((rows, rows), 0) <= iota((rows, rows), 1)
    for g in range(group):
        if g % (group // 2) == 0:
            for copy in copies[:2] if g == 0 else copies[2:]:
                copy.wait()
        s = jnp.where(causal, dot(k, q_ref[:, g * HD : (g + 1) * HD].T) * SCALE2, NEG)
        m = jnp.max(s, axis=0, keepdims=True)
        e = jnp.exp2(s - m)
        dp = dot(v, c_ref[:, g * HD : (g + 1) * HD].T)
        stats_ref[g : g + 1] = m
        stats_ref[group + g : group + g + 1] = jnp.sum(e, axis=0, keepdims=True)
        stats_ref[2 * group + g : 2 * group + g + 1] = jnp.sum(e * dp, axis=0, keepdims=True)
    fetch([(stats_ref, head_of(stats_hbm, stats_ref))], sems.at[pl.ds(5, 1)])[0].wait()


def text_pair(kv_ref):
    a = iota((HD, HD), 0)
    order = one_hot(iota((HD, HD), 1) == 2 * (a & 63) + (a >> 6))
    return split(order, kv_ref)


def split(order, ref):
    keys = []
    values = []
    for b in range(ref.shape[0] // HD):
        part = dot(order, ref[b * HD : (b + 1) * HD]).astype(BF16)
        keys.append(part[:64])
        values.append(part[64:])
    return jnp.concatenate(keys, axis=0), jnp.concatenate(values, axis=0)


def slot_place(j):
    return 4 * ((j & 63) >> 1) + 2 * (j >> 6) + (j & 1)


def slot_pair(in_ref):
    order = one_hot(iota((HD, HD), 1) == slot_place(iota((HD, HD), 0)))
    keys, values = split(order, in_ref)
    live = jnp.broadcast_to(keys[:, :1].astype(F32) < 0.5 * EMPTY, keys.shape)
    bias = jnp.where(live, 0.0, NEG)
    keys = jnp.where(live, keys.astype(F32), 0.0).astype(BF16)
    return keys, values, jnp.concatenate([bias, bias], axis=1)


def slots_kernel(
    in_ref, text_hbm, q_hbm, c_hbm, out_ref, stats_hbm, in_hbm,
    text_ref, q_ref, c_ref, stats_ref, sems,
):
    copies = fetch_wide(q_hbm, c_hbm, q_ref, c_ref, sems.at[pl.ds(1, 4)])
    pairs = [(head_of(text_hbm, text_ref), text_ref)]
    stats = fetch(pairs, sems.at[pl.ds(0, 1)])[0]
    kept = fetch([(in_ref, head_of(in_hbm, in_ref))], sems.at[pl.ds(6, 1)])[0]
    group = q_ref.shape[1] // HD
    k, v, bias = slot_pair(in_ref)
    slots = k.shape[0]
    stats.wait()
    dk = jnp.zeros((slots, HD), F32)
    dv = jnp.zeros((slots, HD), F32)
    for g in range(group):
        if g % (group // 2) == 0:
            for copy in copies[:2] if g == 0 else copies[2:]:
                copy.wait()
        q = q_ref[:, g * HD : (g + 1) * HD]
        c = c_ref[:, g * HD : (g + 1) * HD]
        s = dot(k, q.T) * SCALE2 + bias
        dp = dot(v, c.T)
        mt = text_ref[g : g + 1]
        m = jnp.maximum(mt, jnp.max(s, axis=0, keepdims=True))
        e = jnp.exp2(s - m)
        alpha = jnp.exp2(mt - m)
        total = text_ref[group + g : group + g + 1] * alpha + jnp.sum(e, axis=0, keepdims=True)
        inv = 1.0 / total
        delta = text_ref[2 * group + g : 2 * group + g + 1] * alpha
        delta = (delta + jnp.sum(e * dp, axis=0, keepdims=True)) * inv
        stats_ref[g : g + 1] = m
        stats_ref[group + g : group + g + 1] = inv
        p = e * inv
        ds = (p * (dp - delta)).astype(BF16)
        dk = dk + dot(ds, q)
        dv = dv + dot(p.astype(BF16), c)
    sent = fetch([(stats_ref, head_of(stats_hbm, stats_ref))], sems.at[pl.ds(5, 1)])[0]
    dk = (dk * (1.0 / math.sqrt(HD))).astype(BF16)
    dv = dv.astype(BF16)
    order = one_hot(iota((HD, HD), 0) == slot_place(iota((HD, HD), 1)))
    for b in range(slots // 64):
        pair = jnp.concatenate([dk[b * 64 : (b + 1) * 64], dv[b * 64 : (b + 1) * 64]], axis=0)
        out_ref[b * HD : (b + 1) * HD] = dot(order, pair).astype(BF16)
    sent.wait()
    kept.wait()


def output_kernel(
    in_hbm, kv_hbm, stats_hbm, q_hbm, out_ref, in_ref, kv_ref, stats_ref, q_ref, sems
):
    pairs = [(head_of(in_hbm, in_ref), in_ref), (kv_hbm, kv_ref), (q_hbm, q_ref)]
    pairs += [(head_of(stats_hbm, stats_ref), stats_ref)]
    for copy in fetch(pairs, sems):
        copy.wait()
    group = q_ref.shape[1] // HD
    rows = q_ref.shape[0]
    kt, vt = text_pair(kv_ref)
    ks, vs, bias = slot_pair(in_ref)
    vt = vt.T
    vs = vs.T
    causal = iota((rows, rows), 0) <= iota((rows, rows), 1)
    for g in range(group):
        qt = q_ref[:, g * HD : (g + 1) * HD].T
        m = stats_ref[g : g + 1]
        inv = stats_ref[group + g : group + g + 1]
        s = jnp.where(causal, dot(kt, qt) * SCALE2, NEG)
        o = dot(vt, (jnp.exp2(s - m) * inv).astype(BF16))
        s = dot(ks, qt) * SCALE2 + bias
        o = o + dot(vs, (jnp.exp2(s - m) * inv).astype(BF16))
        out_ref[:, g * HD : (g + 1) * HD] = o.T.astype(BF16)


def rows_kernel(in_ref, code_ref, out_ref):
    code = jnp.broadcast_to(code_ref[:1], (HD, HD)).T
    count = in_ref.shape[0]
    picks = one_hot(iota((HD, count), 1).astype(F32) == code[:, :1])
    g = dot(picks, in_ref[...]).astype(BF16)
    half = HD // 2
    for m in range(4):
        out_ref[m, :, :HD] = g[:half]
        out_ref[m, :, HD:] = g[half:]


def fold_kernel(in_ref, w_ref, out_ref):
    grads = jnp.concatenate([in_ref[h] for h in range(4)], axis=1)
    out_ref[...] = dot(w_ref[...], grads.T).T.astype(BF16)


def exchange(x, axes):
    return lax.all_to_all(x, axes, split_axis=0, concat_axis=0, tiled=True)


def on_device(
    patches, window_index, vit_gain, vit_qkv, vit_proj, merge_gain, piece_rows, piece_dest,
    visual_kv, text_query, text_kv, out_cotangent,
):
    shards = lax.axis_size("sec") * lax.axis_size("dp")
    position = lax.axis_index("mp").astype(jnp.int32).reshape(1)
    points, width_part = patches.shape
    width = vit_qkv.shape[0]
    local = vit_qkv.shape[2]
    rows = text_query.shape[0]
    slots = 2 * shards
    merged_rows = points // 4

    x = lax.all_gather(patches.T, "mp", axis=0, tiled=True)
    wt = jnp.transpose(vit_qkv, (1, 2, 0)).reshape(3 * local, width)
    part, own = call(
        vit_kernel, (shape((4, merged_rows, width)), shape((merged_rows, width))),
        position, vit_gain.reshape(-1, HD), window_index.reshape(1, points), wt, x, vit_proj,
        specs=[SM] + [ANY] * 5, limit=WIDE, flops=10**9, moved=4 * 10**6,
        scratch=[
            pltpu.VMEM((width // HD, HD), BF16), pltpu.VMEM((1, points), jnp.int32),
            pltpu.VMEM((3 * local, width), BF16), pltpu.VMEM((width, points), BF16),
            pltpu.VMEM((local, width), BF16), pltpu.VMEM((3 * local, width), BF16), DMA((5,)),
        ],
    )
    code = call(
        code_kernel, shape((8, HD), F32), piece_rows.reshape(1, -1), piece_dest.reshape(1, -1),
        flops=10**6, moved=10**4,
    )
    summed = exchange(part, "mp")
    w_kv = jnp.transpose(visual_kv.reshape(width, 2, 4, HD), (0, 2, 1, 3)).reshape(width, 8 * HD)
    kv_part = call(
        merge_kernel, shape((4, merged_rows, 2 * HD)),
        summed, own, merge_gain.reshape(1, width), w_kv, flops=2 * 10**8, moved=4 * 10**6,
    )
    kv_terms = exchange(kv_part, "mp")
    group = text_query.shape[1] // HD
    text_rows = text_kv.reshape(2 * rows, HD)
    wide = pltpu.VMEM((rows, group * HD), BF16)
    thin = pltpu.VMEM((2 * rows, HD), BF16)
    tall = shape((4 * rows, rows), F32)
    tall_slots = shape((16 * slots, HD))
    stats = call(
        text_kernel, tall, text_rows, text_query, out_cotangent,
        specs=[ANY] * 3, out_specs=ANY,
        scratch=[thin, wide, wide, pltpu.VMEM((3 * group, rows), F32), DMA((6,))], limit=WIDE,
        flops=10**9, moved=2 * 10**6,
    )
    kv_terms, stats = lax.optimization_barrier((kv_terms, stats))
    outgoing = call(
        pack_kernel, shape((2 * slots, HD)), kv_terms, code, specs=[VM, ANY],
        scratch=[pltpu.VMEM((8, HD), F32), DMA((1,))], flops=2 * 10**7, moved=10**6,
    )
    route = ("dp", "sec")
    incoming = exchange(outgoing.reshape(shards, 4, HD), route).reshape(2 * slots, HD)
    slot_rows = pltpu.VMEM(incoming.shape, BF16)
    grads, stats, kept = call(
        slots_kernel, (shape((2 * slots, HD)), tall, tall_slots),
        incoming, stats, text_query, out_cotangent, specs=[VM, ANY, ANY, ANY],
        out_specs=(VM, ANY, ANY), limit=SLOTL,
        scratch=[
            pltpu.VMEM((3 * group, rows), F32), wide, wide, pltpu.VMEM((2 * group, rows), F32),
            DMA((7,)),
        ],
        flops=10**9, moved=2 * 10**6,
    )
    returned = exchange(grads.reshape(shards, 4, HD), route).reshape(2 * slots, HD)
    attended = call(
        output_kernel, shape((rows, group * HD)), kept, text_rows, stats, text_query, specs=[ANY] * 4,
        scratch=[slot_rows, thin, pltpu.VMEM((2 * group, rows), F32), wide, DMA((4,))],
        limit=WIDE, flops=10**9, moved=2 * 10**6,
    )
    returned, attended = lax.optimization_barrier((returned, attended))
    row_grads = call(
        rows_kernel, shape((4, merged_rows, 2 * HD)), returned, code, flops=2 * 10**7, moved=5 * 10**5,
    )
    heads = exchange(row_grads, "mp")
    visual_grad = call(
        fold_kernel, shape((merged_rows, width)), heads, w_kv, flops=2 * 10**8, moved=3 * 10**6,
    )
    return (attended, visual_grad)


def solution(mesh):
    both = ("sec", "dp")
    in_specs = (
        P(both, "mp"), P(both), P(), P(None, None, "mp"), P("mp", None), P(), P(both), P(both),
        P("mp", None, None), P(both, "mp"), P(both, None, "mp"), P(both, "mp"),
    )
    return jax.shard_map(
        on_device, mesh=mesh, in_specs=in_specs, out_specs=(P(both, "mp"), P(both, "mp")),
        check_vma=False,
    )
```

```python
import math

import jax
import jax.numpy as jnp
from jax import lax
from jax.experimental import pallas as pl
from jax.experimental.pallas import tpu as pltpu
from jax.sharding import PartitionSpec as P

VIT_HD = 80
HD = 128
EPS = 1e-6
NEG = -1e30
EMPTY = 2.0**100
WIDE = 59
DP = 64
SLOTL = 53.5
LOG2E = math.log2(math.e)
SCALE2 = LOG2E / math.sqrt(HD)
F32 = jnp.float32
BF16 = jnp.bfloat16
VM = pl.BlockSpec(memory_space=pltpu.VMEM)
SM = pl.BlockSpec(memory_space=pltpu.SMEM)
ANY = pl.BlockSpec(memory_space=pl.ANY)
DMA = pltpu.SemaphoreType.DMA


def dot(a, b):
    return jnp.dot(a, b, preferred_element_type=F32)


def iota(shape, dim):
    return lax.broadcasted_iota(jnp.int32, shape, dim)


def call(kernel, out_shape, *args, flops=0, moved=0, limit=6, specs=None, out_specs=None, scratch=()):
    return pl.pallas_call(
        kernel,
        out_shape=out_shape,
        in_specs=specs or [VM] * len(args),
        out_specs=out_specs or jax.tree.map(lambda _: VM, out_shape),
        scratch_shapes=scratch,
        compiler_params=limit and pltpu.CompilerParams(vmem_limit_bytes=int(limit * 2**20)),
        cost_estimate=pl.CostEstimate(flops=flops, bytes_accessed=moved, transcendentals=0),
    )(*args)


def shape(dims, dtype=BF16):
    return jax.ShapeDtypeStruct(dims, dtype)


def one_hot(mask):
    return mask.astype(F32).astype(BF16)


def fetch(pairs, sems):
    copies = [pltpu.make_async_copy(a, b, sems.at[i]) for i, (a, b) in enumerate(pairs)]
    for copy in copies:
        copy.start()
    return copies


def code_kernel(rows_ref, dest_ref, code_ref):
    pieces = rows_ref.shape[1]
    a = iota((pieces, pieces), 0)
    b = iota((pieces, pieces), 1)
    rows = jnp.broadcast_to(rows_ref[...].astype(F32), (pieces, pieces))
    place = dest_ref[...]
    place = (place & (DP - 1)) * 2 + (place >> (DP.bit_length() - 1))
    dest = jnp.broadcast_to(place.astype(F32), (pieces, pieces))
    starts = jnp.sum(jnp.where(b < a, rows, 0.0), axis=1, keepdims=True)
    count = jnp.sum(jnp.where(b == a, rows, 0.0), axis=1, keepdims=True)
    target = jnp.sum(jnp.where(b == a, dest, 0.0), axis=1, keepdims=True)
    lane = iota((pieces, HD), 1)
    row = (lane & 63).astype(F32)
    inside = (row >= starts) & (row < starts + count)
    code = jnp.sum(jnp.where(inside, target * 4.0 + row - starts, 0.0), axis=0, keepdims=True)
    code_ref[...] = jnp.broadcast_to(code, (8, HD)) + 2.0 * (iota((8, HD), 1) >> 6).astype(F32)


def vit_kernel(
    pos_ref, gain_hbm, win_hbm, wt_hbm, x_hbm, proj_hbm, part_ref, own_ref,
    gain_ref, win_ref, wt_ref, x_ref, proj_ref, w_ref, sems,
):
    pairs = [(gain_hbm, gain_ref), (x_hbm, x_ref), (wt_hbm, wt_ref)]
    pairs += [(win_hbm, win_ref), (proj_hbm, proj_ref)]
    copies = fetch(pairs, sems)
    width, points = x_ref.shape
    copies[0].wait()
    copies[1].wait()
    x = x_ref[...]
    local = proj_ref.shape[0]
    xf = x.astype(F32)
    scale = lax.rsqrt(jnp.sum(xf * xf, axis=0, keepdims=True) * (1.0 / width) + EPS)
    copies[2].wait()
    for i in range(width // HD):
        cols = slice(i * HD, (i + 1) * HD)
        w_ref[:, cols] = (wt_ref[:, cols].astype(F32) * gain_ref[i : i + 1].astype(F32)).astype(BF16)
    qkv = (dot(w_ref[...], x) * scale).astype(BF16)
    copies[3].wait()
    wins = jnp.broadcast_to(win_ref[...].astype(F32), (8, points))
    bias = jnp.where(wins.T[:, :1] == wins[:1], 0.0, NEG)
    mixed = []
    for h in range(local // VIT_HD):
        q = qkv[h * VIT_HD : (h + 1) * VIT_HD]
        k = qkv[local + h * VIT_HD : local + (h + 1) * VIT_HD]
        v = qkv[2 * local + h * VIT_HD : 2 * local + (h + 1) * VIT_HD]
        s = dot(k.T, q) * (LOG2E / math.sqrt(VIT_HD)) + bias
        e = jnp.exp2(s - jnp.max(s, axis=0, keepdims=True))
        weights = (e * (1.0 / jnp.sum(e, axis=0, keepdims=True))).astype(BF16)
        mixed.append(dot(v, weights).astype(BF16))
    mixed = jnp.concatenate(mixed, axis=0)
    n = iota((points, points), 1)
    perm = one_hot(iota((points, points), 0) == 4 * (n & 63) + (n >> 6))
    mixed = dot(mixed, perm).astype(BF16)
    copies[4].wait()
    part = dot(mixed.T, proj_ref[...]).astype(BF16)
    for m in range(4):
        part_ref[m] = part[m * 64 : (m + 1) * 64]
    sel = one_hot(iota((points, 64), 0) == 4 * iota((points, 64), 1) + pos_ref[0])
    own_ref[...] = dot(x, sel).astype(BF16).T


def merge_kernel(in_ref, own_ref, gain_ref, w_ref, out_ref):
    resid = own_ref[...].astype(F32)
    for m in range(4):
        resid = resid + in_ref[m].astype(F32)
    scale = lax.rsqrt(jnp.mean(resid * resid, axis=1, keepdims=True) + EPS)
    merged = (resid * scale * gain_ref[...].astype(F32)).astype(BF16)
    kv = dot(merged, w_ref[...]).astype(BF16)
    for h in range(4):
        out_ref[h] = kv[:, h * 256 : (h + 1) * 256]


def pack_kernel(in_ref, code_hbm, out_ref, code_ref, sems):
    copies = fetch([(code_hbm, code_ref)], sems)
    kv = in_ref[0].astype(F32)
    for m in range(1, 4):
        kv = kv + in_ref[m].astype(F32)
    kv = kv.astype(BF16)
    stack = jnp.concatenate([kv[:, :HD], kv[:, HD:]], axis=0)
    copies[0].wait()
    dims = out_ref.shape
    row = iota(dims, 0)
    picks = one_hot(row.astype(F32) == code_ref[:1])
    filled = dot(picks, jnp.ones((HD, HD), BF16))
    empty = jnp.where(((row & 2) == 0) & (filled < 0.5), EMPTY, 0.0)
    out_ref[...] = (dot(picks, stack) + empty).astype(BF16)


def head_of(tall, ref):
    return tall.at[pl.ds(0, ref.shape[0])]


def halves(ref):
    half = ref.shape[1] // 2
    return [ref.at[:, :half], ref.at[:, half:]]


def fetch_wide(q_hbm, c_hbm, q_ref, c_ref, sems):
    pairs = list(zip(halves(q_hbm) + halves(c_hbm), halves(q_ref) + halves(c_ref)))
    q0, q1, c0, c1 = pairs
    return fetch([q0, c0, q1, c1], sems)


def text_kernel(kv_hbm, q_hbm, c_hbm, stats_hbm, kv_ref, q_ref, c_ref, stats_ref, sems):
    head = fetch([(kv_hbm, kv_ref)], sems.at[pl.ds(0, 1)])[0]
    copies = fetch_wide(q_hbm, c_hbm, q_ref, c_ref, sems.at[pl.ds(1, 4)])
    group = q_ref.shape[1] // HD
    rows = q_ref.shape[0]
    head.wait()
    k, v = text_pair(kv_ref)
    causal = iota((rows, rows), 0) <= iota((rows, rows), 1)
    for g in range(group):
        if g % (group // 2) == 0:
            for copy in copies[:2] if g == 0 else copies[2:]:
                copy.wait()
        s = jnp.where(causal, dot(k, q_ref[:, g * HD : (g + 1) * HD].T) * SCALE2, NEG)
        m = jnp.max(s, axis=0, keepdims=True)
        e = jnp.exp2(s - m)
        dp = dot(v, c_ref[:, g * HD : (g + 1) * HD].T)
        stats_ref[g : g + 1] = m
        stats_ref[group + g : group + g + 1] = jnp.sum(e, axis=0, keepdims=True)
        stats_ref[2 * group + g : 2 * group + g + 1] = jnp.sum(e * dp, axis=0, keepdims=True)
    fetch([(stats_ref, head_of(stats_hbm, stats_ref))], sems.at[pl.ds(5, 1)])[0].wait()


def text_pair(kv_ref):
    a = iota((HD, HD), 0)
    order = one_hot(iota((HD, HD), 1) == 2 * (a & 63) + (a >> 6))
    return split(order, kv_ref)


def split(order, ref):
    keys = []
    values = []
    for b in range(ref.shape[0] // HD):
        part = dot(order, ref[b * HD : (b + 1) * HD]).astype(BF16)
        keys.append(part[:64])
        values.append(part[64:])
    return jnp.concatenate(keys, axis=0), jnp.concatenate(values, axis=0)


def slot_place(j):
    return 4 * ((j & 63) >> 1) + 2 * (j >> 6) + (j & 1)


def slot_pair(in_ref):
    order = one_hot(iota((HD, HD), 1) == slot_place(iota((HD, HD), 0)))
    keys, values = split(order, in_ref)
    live = jnp.broadcast_to(keys[:, :1].astype(F32) < 0.5 * EMPTY, keys.shape)
    bias = jnp.where(live, 0.0, NEG)
    keys = jnp.where(live, keys.astype(F32), 0.0).astype(BF16)
    return keys, values, jnp.concatenate([bias, bias], axis=1)


def slots_kernel(
    in_ref, text_hbm, q_hbm, c_hbm, out_ref, stats_hbm, in_hbm,
    text_ref, q_ref, c_ref, stats_ref, sems,
):
    copies = fetch_wide(q_hbm, c_hbm, q_ref, c_ref, sems.at[pl.ds(1, 4)])
    pairs = [(head_of(text_hbm, text_ref), text_ref)]
    stats = fetch(pairs, sems.at[pl.ds(0, 1)])[0]
    kept = fetch([(in_ref, head_of(in_hbm, in_ref))], sems.at[pl.ds(6, 1)])[0]
    group = q_ref.shape[1] // HD
    k, v, bias = slot_pair(in_ref)
    slots = k.shape[0]
    stats.wait()
    dk = jnp.zeros((slots, HD), F32)
    dv = jnp.zeros((slots, HD), F32)
    held = [[], [], [], []]
    for g in range(group):
        if g % (group // 2) == 0:
            for copy in copies[:2] if g == 0 else copies[2:]:
                copy.wait()
        q = q_ref[:, g * HD : (g + 1) * HD]
        c = c_ref[:, g * HD : (g + 1) * HD]
        s = dot(k, q.T) * SCALE2 + bias
        dp = dot(v, c.T)
        mt = text_ref[g : g + 1]
        m = jnp.maximum(mt, jnp.max(s, axis=0, keepdims=True))
        e = jnp.exp2(s - m)
        alpha = jnp.exp2(mt - m)
        total = text_ref[group + g : group + g + 1] * alpha + jnp.sum(e, axis=0, keepdims=True)
        inv = 1.0 / total
        delta = text_ref[2 * group + g : 2 * group + g + 1] * alpha
        delta = (delta + jnp.sum(e * dp, axis=0, keepdims=True)) * inv
        stats_ref[g : g + 1] = m
        stats_ref[group + g : group + g + 1] = inv
        p = e * inv
        lists = ((p * (dp - delta)).astype(BF16), p.astype(BF16), q, c)
        for some, one in zip(held, lists):
            some.append(one)
        if g % (group // 2) == group // 2 - 1:
            ds, ps = (jnp.concatenate(some, axis=1) for some in held[:2])
            qs, cs = (jnp.concatenate(some, axis=0) for some in held[2:])
            dk = dk + dot(ds, qs)
            dv = dv + dot(ps, cs)
            held = [[], [], [], []]
    sent = fetch([(stats_ref, head_of(stats_hbm, stats_ref))], sems.at[pl.ds(5, 1)])[0]
    dk = (dk * (1.0 / math.sqrt(HD))).astype(BF16)
    dv = dv.astype(BF16)
    order = one_hot(iota((HD, HD), 0) == slot_place(iota((HD, HD), 1)))
    for b in range(slots // 64):
        pair = jnp.concatenate([dk[b * 64 : (b + 1) * 64], dv[b * 64 : (b + 1) * 64]], axis=0)
        out_ref[b * HD : (b + 1) * HD] = dot(order, pair).astype(BF16)
    sent.wait()
    kept.wait()


def output_kernel(
    in_hbm, kv_hbm, stats_hbm, q_hbm, out_ref, in_ref, kv_ref, stats_ref, q_ref, sems
):
    pairs = [(head_of(in_hbm, in_ref), in_ref), (kv_hbm, kv_ref), (q_hbm, q_ref)]
    pairs += [(head_of(stats_hbm, stats_ref), stats_ref)]
    for copy in fetch(pairs, sems):
        copy.wait()
    group = q_ref.shape[1] // HD
    rows = q_ref.shape[0]
    kt, vt = text_pair(kv_ref)
    ks, vs, bias = slot_pair(in_ref)
    values = jnp.concatenate([vt, vs], axis=0).T
    causal = iota((rows, rows), 0) <= iota((rows, rows), 1)
    for g in range(group):
        qt = q_ref[:, g * HD : (g + 1) * HD].T
        m = stats_ref[g : g + 1]
        inv = stats_ref[group + g : group + g + 1]
        text = jnp.where(causal, dot(kt, qt) * SCALE2, NEG)
        slot = dot(ks, qt) * SCALE2 + bias
        s = jnp.concatenate([text, slot], axis=0)
        o = dot(values, (jnp.exp2(s - m) * inv).astype(BF16))
        out_ref[:, g * HD : (g + 1) * HD] = o.T.astype(BF16)


def rows_kernel(in_ref, code_ref, out_ref):
    code = jnp.broadcast_to(code_ref[:1], (HD, HD)).T
    count = in_ref.shape[0]
    picks = one_hot(iota((HD, count), 1).astype(F32) == code[:, :1])
    g = dot(picks, in_ref[...]).astype(BF16)
    half = HD // 2
    for m in range(4):
        out_ref[m, :, :HD] = g[:half]
        out_ref[m, :, HD:] = g[half:]


def fold_kernel(in_ref, w_ref, out_ref):
    grads = jnp.concatenate([in_ref[h] for h in range(4)], axis=1)
    out_ref[...] = dot(w_ref[...], grads.T).T.astype(BF16)


def exchange(x, axes):
    return lax.all_to_all(x, axes, split_axis=0, concat_axis=0, tiled=True)


def on_device(
    patches, window_index, vit_gain, vit_qkv, vit_proj, merge_gain, piece_rows, piece_dest,
    visual_kv, text_query, text_kv, out_cotangent,
):
    shards = lax.axis_size("sec") * lax.axis_size("dp")
    position = lax.axis_index("mp").astype(jnp.int32).reshape(1)
    points, width_part = patches.shape
    width = vit_qkv.shape[0]
    local = vit_qkv.shape[2]
    rows = text_query.shape[0]
    slots = 2 * shards
    merged_rows = points // 4

    x = lax.all_gather(patches.T, "mp", axis=0, tiled=True)
    wt = jnp.transpose(vit_qkv, (1, 2, 0)).reshape(3 * local, width)
    part, own = call(
        vit_kernel, (shape((4, merged_rows, width)), shape((merged_rows, width))),
        position, vit_gain.reshape(-1, HD), window_index.reshape(1, points), wt, x, vit_proj,
        specs=[SM] + [ANY] * 5, limit=WIDE, flops=10**9, moved=4 * 10**6,
        scratch=[
            pltpu.VMEM((width // HD, HD), BF16), pltpu.VMEM((1, points), jnp.int32),
            pltpu.VMEM((3 * local, width), BF16), pltpu.VMEM((width, points), BF16),
            pltpu.VMEM((local, width), BF16), pltpu.VMEM((3 * local, width), BF16), DMA((5,)),
        ],
    )
    code = call(
        code_kernel, shape((8, HD), F32), piece_rows.reshape(1, -1), piece_dest.reshape(1, -1),
        flops=10**6, moved=10**4,
    )
    summed = exchange(part, "mp")
    w_kv = jnp.transpose(visual_kv.reshape(width, 2, 4, HD), (0, 2, 1, 3)).reshape(width, 8 * HD)
    kv_part = call(
        merge_kernel, shape((4, merged_rows, 2 * HD)),
        summed, own, merge_gain.reshape(1, width), w_kv, flops=2 * 10**8, moved=4 * 10**6,
    )
    kv_terms = exchange(kv_part, "mp")
    group = text_query.shape[1] // HD
    text_rows = text_kv.reshape(2 * rows, HD)
    wide = pltpu.VMEM((rows, group * HD), BF16)
    thin = pltpu.VMEM((2 * rows, HD), BF16)
    tall = shape((4 * rows, rows), F32)
    tall_slots = shape((16 * slots, HD))
    stats = call(
        text_kernel, tall, text_rows, text_query, out_cotangent,
        specs=[ANY] * 3, out_specs=ANY,
        scratch=[thin, wide, wide, pltpu.VMEM((3 * group, rows), F32), DMA((6,))], limit=WIDE,
        flops=10**9, moved=2 * 10**6,
    )
    kv_terms, stats = lax.optimization_barrier((kv_terms, stats))
    outgoing = call(
        pack_kernel, shape((2 * slots, HD)), kv_terms, code, specs=[VM, ANY],
        scratch=[pltpu.VMEM((8, HD), F32), DMA((1,))], flops=2 * 10**7, moved=10**6,
    )
    route = ("dp", "sec")
    incoming = exchange(outgoing.reshape(shards, 4, HD), route).reshape(2 * slots, HD)
    slot_rows = pltpu.VMEM(incoming.shape, BF16)
    grads, stats, kept = call(
        slots_kernel, (shape((2 * slots, HD)), tall, tall_slots),
        incoming, stats, text_query, out_cotangent, specs=[VM, ANY, ANY, ANY],
        out_specs=(VM, ANY, ANY), limit=SLOTL,
        scratch=[
            pltpu.VMEM((3 * group, rows), F32), wide, wide, pltpu.VMEM((2 * group, rows), F32),
            DMA((7,)),
        ],
        flops=10**9, moved=2 * 10**6,
    )
    returned = exchange(grads.reshape(shards, 4, HD), route).reshape(2 * slots, HD)
    attended = call(
        output_kernel, shape((rows, group * HD)), kept, text_rows, stats, text_query, specs=[ANY] * 4,
        scratch=[slot_rows, thin, pltpu.VMEM((2 * group, rows), F32), wide, DMA((4,))],
        limit=WIDE, flops=10**9, moved=2 * 10**6,
    )
    returned, attended = lax.optimization_barrier((returned, attended))
    row_grads = call(
        rows_kernel, shape((4, merged_rows, 2 * HD)), returned, code, flops=2 * 10**7, moved=5 * 10**5,
    )
    heads = exchange(row_grads, "mp")
    visual_grad = call(
        fold_kernel, shape((merged_rows, width)), heads, w_kv, flops=2 * 10**8, moved=3 * 10**6,
    )
    return (attended, visual_grad)


def solution(mesh):
    both = ("sec", "dp")
    in_specs = (
        P(both, "mp"), P(both), P(), P(None, None, "mp"), P("mp", None), P(), P(both), P(both),
        P("mp", None, None), P(both, "mp"), P(both, None, "mp"), P(both, "mp"),
    )
    return jax.shard_map(
        on_device, mesh=mesh, in_specs=in_specs, out_specs=(P(both, "mp"), P(both, "mp")),
        check_vma=False,
    )
```

```python
import math

import jax
import jax.numpy as jnp
from jax import lax
from jax.experimental import pallas as pl
from jax.experimental.pallas import tpu as pltpu
from jax.sharding import PartitionSpec as P

VIT_HD = 80
HD = 128
EPS = 1e-6
NEG = -1e30
EMPTY = 2.0**100
WIDE = 59
DP = 64
SLOTL = 53.5
LOG2E = math.log2(math.e)
SCALE2 = LOG2E / math.sqrt(HD)
F32 = jnp.float32
BF16 = jnp.bfloat16
VM = pl.BlockSpec(memory_space=pltpu.VMEM)
SM = pl.BlockSpec(memory_space=pltpu.SMEM)
ANY = pl.BlockSpec(memory_space=pl.ANY)
DMA = pltpu.SemaphoreType.DMA


def dot(a, b):
    return jnp.dot(a, b, preferred_element_type=F32)


def iota(shape, dim):
    return lax.broadcasted_iota(jnp.int32, shape, dim)


def call(kernel, out_shape, *args, flops=0, moved=0, limit=6, specs=None, out_specs=None, scratch=()):
    return pl.pallas_call(
        kernel,
        out_shape=out_shape,
        in_specs=specs or [VM] * len(args),
        out_specs=out_specs or jax.tree.map(lambda _: VM, out_shape),
        scratch_shapes=scratch,
        compiler_params=limit and pltpu.CompilerParams(vmem_limit_bytes=int(limit * 2**20)),
        cost_estimate=pl.CostEstimate(flops=flops, bytes_accessed=moved, transcendentals=0),
    )(*args)


def shape(dims, dtype=BF16):
    return jax.ShapeDtypeStruct(dims, dtype)


def one_hot(mask):
    return mask.astype(F32).astype(BF16)


def fetch(pairs, sems):
    copies = [pltpu.make_async_copy(a, b, sems.at[i]) for i, (a, b) in enumerate(pairs)]
    for copy in copies:
        copy.start()
    return copies


def code_kernel(rows_ref, dest_ref, code_ref):
    pieces = rows_ref.shape[1]
    a = iota((pieces, pieces), 0)
    b = iota((pieces, pieces), 1)
    rows = jnp.broadcast_to(rows_ref[...].astype(F32), (pieces, pieces))
    place = dest_ref[...]
    place = (place & (DP - 1)) * 2 + (place >> (DP.bit_length() - 1))
    dest = jnp.broadcast_to(place.astype(F32), (pieces, pieces))
    starts = jnp.sum(jnp.where(b < a, rows, 0.0), axis=1, keepdims=True)
    count = jnp.sum(jnp.where(b == a, rows, 0.0), axis=1, keepdims=True)
    target = jnp.sum(jnp.where(b == a, dest, 0.0), axis=1, keepdims=True)
    lane = iota((pieces, HD), 1)
    row = (lane & 63).astype(F32)
    inside = (row >= starts) & (row < starts + count)
    code = jnp.sum(jnp.where(inside, target * 4.0 + row - starts, 0.0), axis=0, keepdims=True)
    code_ref[...] = jnp.broadcast_to(code, (8, HD)) + 2.0 * (iota((8, HD), 1) >> 6).astype(F32)


def vit_kernel(
    pos_ref, gain_hbm, win_hbm, wt_hbm, x_hbm, proj_hbm, part_ref, own_ref,
    gain_ref, win_ref, wt_ref, x_ref, proj_ref, w_ref, sems,
):
    pairs = [(gain_hbm, gain_ref), (x_hbm, x_ref), (wt_hbm, wt_ref)]
    pairs += [(win_hbm, win_ref), (proj_hbm, proj_ref)]
    copies = fetch(pairs, sems)
    width, points = x_ref.shape
    copies[0].wait()
    copies[1].wait()
    x = x_ref[...]
    local = proj_ref.shape[0]
    xf = x.astype(F32)
    scale = lax.rsqrt(jnp.sum(xf * xf, axis=0, keepdims=True) * (1.0 / width) + EPS)
    copies[2].wait()
    for i in range(width // HD):
        cols = slice(i * HD, (i + 1) * HD)
        w_ref[:, cols] = (wt_ref[:, cols].astype(F32) * gain_ref[i : i + 1].astype(F32)).astype(BF16)
    qkv = (dot(w_ref[...], x) * scale).astype(BF16)
    copies[3].wait()
    wins = jnp.broadcast_to(win_ref[...].astype(F32), (8, points))
    bias = jnp.where(wins.T[:, :1] == wins[:1], 0.0, NEG)
    mixed = []
    for h in range(local // VIT_HD):
        q = qkv[h * VIT_HD : (h + 1) * VIT_HD]
        k = qkv[local + h * VIT_HD : local + (h + 1) * VIT_HD]
        v = qkv[2 * local + h * VIT_HD : 2 * local + (h + 1) * VIT_HD]
        s = dot(k.T, q) * (LOG2E / math.sqrt(VIT_HD)) + bias
        e = jnp.exp2(s - jnp.max(s, axis=0, keepdims=True))
        weights = (e * (1.0 / jnp.sum(e, axis=0, keepdims=True))).astype(BF16)
        mixed.append(dot(v, weights).astype(BF16))
    mixed = jnp.concatenate(mixed, axis=0)
    n = iota((points, points), 1)
    perm = one_hot(iota((points, points), 0) == 4 * (n & 63) + (n >> 6))
    mixed = dot(mixed, perm).astype(BF16)
    copies[4].wait()
    part = dot(mixed.T, proj_ref[...]).astype(BF16)
    for m in range(4):
        part_ref[m] = part[m * 64 : (m + 1) * 64]
    sel = one_hot(iota((points, 64), 0) == 4 * iota((points, 64), 1) + pos_ref[0])
    own_ref[...] = dot(x, sel).astype(BF16).T


def merge_kernel(in_ref, own_ref, gain_ref, w_ref, out_ref):
    resid = own_ref[...].astype(F32)
    for m in range(4):
        resid = resid + in_ref[m].astype(F32)
    scale = lax.rsqrt(jnp.mean(resid * resid, axis=1, keepdims=True) + EPS)
    merged = (resid * scale * gain_ref[...].astype(F32)).astype(BF16)
    kv = dot(merged, w_ref[...]).astype(BF16)
    for h in range(4):
        out_ref[h] = kv[:, h * 256 : (h + 1) * 256]


def pack_kernel(in_ref, code_hbm, out_ref, code_ref, sems):
    copies = fetch([(code_hbm, code_ref)], sems)
    kv = in_ref[0].astype(F32)
    for m in range(1, 4):
        kv = kv + in_ref[m].astype(F32)
    kv = kv.astype(BF16)
    stack = jnp.concatenate([kv[:, :HD], kv[:, HD:]], axis=0)
    copies[0].wait()
    dims = out_ref.shape
    row = iota(dims, 0)
    picks = one_hot(row.astype(F32) == code_ref[:1])
    filled = dot(picks, jnp.ones((HD, HD), BF16))
    empty = jnp.where(((row & 2) == 0) & (filled < 0.5), EMPTY, 0.0)
    out_ref[...] = (dot(picks, stack) + empty).astype(BF16)


def head_of(tall, ref):
    return tall.at[pl.ds(0, ref.shape[0])]


def text_kernel(kv_hbm, q_hbm, c_hbm, stats_hbm, kv_ref, q_ref, c_ref, stats_ref, sems):
    head = fetch([(kv_hbm, kv_ref)], sems.at[pl.ds(0, 1)])[0]
    copies = fetch([(q_hbm, q_ref), (c_hbm, c_ref)], sems.at[pl.ds(1, 2)])
    group = q_ref.shape[1] // HD
    rows = q_ref.shape[0]
    head.wait()
    k, v = text_pair(kv_ref)
    causal = iota((rows, rows), 0) <= iota((rows, rows), 1)
    for g in range(group):
        if g == 0:
            for copy in copies:
                copy.wait()
        s = jnp.where(causal, dot(k, q_ref[:, g * HD : (g + 1) * HD].T) * SCALE2, NEG)
        m = jnp.max(s, axis=0, keepdims=True)
        e = jnp.exp2(s - m)
        dp = dot(v, c_ref[:, g * HD : (g + 1) * HD].T)
        stats_ref[g : g + 1] = m
        stats_ref[group + g : group + g + 1] = jnp.sum(e, axis=0, keepdims=True)
        stats_ref[2 * group + g : 2 * group + g + 1] = jnp.sum(e * dp, axis=0, keepdims=True)
    fetch([(stats_ref, head_of(stats_hbm, stats_ref))], sems.at[pl.ds(3, 1)])[0].wait()


def text_pair(kv_ref):
    a = iota((HD, HD), 0)
    order = one_hot(iota((HD, HD), 1) == 2 * (a & 63) + (a >> 6))
    return split(order, kv_ref)


def split(order, ref):
    keys = []
    values = []
    for b in range(ref.shape[0] // HD):
        part = dot(order, ref[b * HD : (b + 1) * HD]).astype(BF16)
        keys.append(part[:64])
        values.append(part[64:])
    return jnp.concatenate(keys, axis=0), jnp.concatenate(values, axis=0)


def slot_place(j):
    return 4 * ((j & 63) >> 1) + 2 * (j >> 6) + (j & 1)


def slot_pair(in_ref):
    order = one_hot(iota((HD, HD), 1) == slot_place(iota((HD, HD), 0)))
    keys, values = split(order, in_ref)
    live = jnp.broadcast_to(keys[:, :1].astype(F32) < 0.5 * EMPTY, keys.shape)
    bias = jnp.where(live, 0.0, NEG)
    keys = jnp.where(live, keys.astype(F32), 0.0).astype(BF16)
    return keys, values, jnp.concatenate([bias, bias], axis=1)


def slots_kernel(
    in_ref, text_hbm, q_hbm, c_hbm, out_ref, stats_hbm, in_hbm,
    text_ref, q_ref, c_ref, stats_ref, sems,
):
    copies = fetch([(q_hbm, q_ref), (c_hbm, c_ref)], sems.at[pl.ds(1, 2)])
    pairs = [(head_of(text_hbm, text_ref), text_ref)]
    stats = fetch(pairs, sems.at[pl.ds(0, 1)])[0]
    kept = fetch([(in_ref, head_of(in_hbm, in_ref))], sems.at[pl.ds(4, 1)])[0]
    group = q_ref.shape[1] // HD
    k, v, bias = slot_pair(in_ref)
    slots = k.shape[0]
    stats.wait()
    dk = jnp.zeros((slots, HD), F32)
    dv = jnp.zeros((slots, HD), F32)
    held = [[], [], [], []]
    for g in range(group):
        if g == 0:
            for copy in copies:
                copy.wait()
        q = q_ref[:, g * HD : (g + 1) * HD]
        c = c_ref[:, g * HD : (g + 1) * HD]
        s = dot(k, q.T) * SCALE2 + bias
        dp = dot(v, c.T)
        mt = text_ref[g : g + 1]
        m = jnp.maximum(mt, jnp.max(s, axis=0, keepdims=True))
        e = jnp.exp2(s - m)
        alpha = jnp.exp2(mt - m)
        total = text_ref[group + g : group + g + 1] * alpha + jnp.sum(e, axis=0, keepdims=True)
        inv = 1.0 / total
        delta = text_ref[2 * group + g : 2 * group + g + 1] * alpha
        delta = (delta + jnp.sum(e * dp, axis=0, keepdims=True)) * inv
        stats_ref[g : g + 1] = m
        stats_ref[group + g : group + g + 1] = inv
        p = e * inv
        lists = ((p * (dp - delta)).astype(BF16), p.astype(BF16), q, c)
        for some, one in zip(held, lists):
            some.append(one)
        if g % (group // 2) == group // 2 - 1:
            ds, ps = (jnp.concatenate(some, axis=1) for some in held[:2])
            qs, cs = (jnp.concatenate(some, axis=0) for some in held[2:])
            dk = dk + dot(ds, qs)
            dv = dv + dot(ps, cs)
            held = [[], [], [], []]
    sent = fetch([(stats_ref, head_of(stats_hbm, stats_ref))], sems.at[pl.ds(3, 1)])[0]
    dk = (dk * (1.0 / math.sqrt(HD))).astype(BF16)
    dv = dv.astype(BF16)
    order = one_hot(iota((HD, HD), 0) == slot_place(iota((HD, HD), 1)))
    for b in range(slots // 64):
        pair = jnp.concatenate([dk[b * 64 : (b + 1) * 64], dv[b * 64 : (b + 1) * 64]], axis=0)
        out_ref[b * HD : (b + 1) * HD] = dot(order, pair).astype(BF16)
    sent.wait()
    kept.wait()


def output_kernel(
    in_hbm, kv_hbm, stats_hbm, q_hbm, out_ref, in_ref, kv_ref, stats_ref, q_ref, sems
):
    pairs = [(head_of(in_hbm, in_ref), in_ref), (kv_hbm, kv_ref), (q_hbm, q_ref)]
    pairs += [(head_of(stats_hbm, stats_ref), stats_ref)]
    for copy in fetch(pairs, sems):
        copy.wait()
    group = q_ref.shape[1] // HD
    rows = q_ref.shape[0]
    kt, vt = text_pair(kv_ref)
    ks, vs, bias = slot_pair(in_ref)
    values = jnp.concatenate([vt, vs], axis=0).T
    causal = iota((rows, rows), 0) <= iota((rows, rows), 1)
    for g in range(group):
        qt = q_ref[:, g * HD : (g + 1) * HD].T
        m = stats_ref[g : g + 1]
        inv = stats_ref[group + g : group + g + 1]
        text = jnp.where(causal, dot(kt, qt) * SCALE2, NEG)
        slot = dot(ks, qt) * SCALE2 + bias
        s = jnp.concatenate([text, slot], axis=0)
        o = dot(values, (jnp.exp2(s - m) * inv).astype(BF16))
        out_ref[:, g * HD : (g + 1) * HD] = o.T.astype(BF16)


def rows_kernel(in_ref, code_ref, out_ref):
    code = jnp.broadcast_to(code_ref[:1], (HD, HD)).T
    count = in_ref.shape[0]
    picks = one_hot(iota((HD, count), 1).astype(F32) == code[:, :1])
    g = dot(picks, in_ref[...]).astype(BF16)
    half = HD // 2
    for m in range(4):
        out_ref[m, :, :HD] = g[:half]
        out_ref[m, :, HD:] = g[half:]


def fold_kernel(in_ref, w_ref, out_ref):
    grads = jnp.concatenate([in_ref[h] for h in range(4)], axis=1)
    out_ref[...] = dot(w_ref[...], grads.T).T.astype(BF16)


def exchange(x, axes):
    return lax.all_to_all(x, axes, split_axis=0, concat_axis=0, tiled=True)


def on_device(
    patches, window_index, vit_gain, vit_qkv, vit_proj, merge_gain, piece_rows, piece_dest,
    visual_kv, text_query, text_kv, out_cotangent,
):
    shards = lax.axis_size("sec") * lax.axis_size("dp")
    position = lax.axis_index("mp").astype(jnp.int32).reshape(1)
    points, width_part = patches.shape
    width = vit_qkv.shape[0]
    local = vit_qkv.shape[2]
    rows = text_query.shape[0]
    slots = 2 * shards
    merged_rows = points // 4

    x = lax.all_gather(patches.T, "mp", axis=0, tiled=True)
    wt = jnp.transpose(vit_qkv, (1, 2, 0)).reshape(3 * local, width)
    part, own = call(
        vit_kernel, (shape((4, merged_rows, width)), shape((merged_rows, width))),
        position, vit_gain.reshape(-1, HD), window_index.reshape(1, points), wt, x, vit_proj,
        specs=[SM] + [ANY] * 5, limit=WIDE, flops=10**9, moved=4 * 10**6,
        scratch=[
            pltpu.VMEM((width // HD, HD), BF16), pltpu.VMEM((1, points), jnp.int32),
            pltpu.VMEM((3 * local, width), BF16), pltpu.VMEM((width, points), BF16),
            pltpu.VMEM((local, width), BF16), pltpu.VMEM((3 * local, width), BF16), DMA((5,)),
        ],
    )
    code = call(
        code_kernel, shape((8, HD), F32), piece_rows.reshape(1, -1), piece_dest.reshape(1, -1),
        flops=10**6, moved=10**4,
    )
    summed = exchange(part, "mp")
    w_kv = jnp.transpose(visual_kv.reshape(width, 2, 4, HD), (0, 2, 1, 3)).reshape(width, 8 * HD)
    kv_part = call(
        merge_kernel, shape((4, merged_rows, 2 * HD)),
        summed, own, merge_gain.reshape(1, width), w_kv, flops=2 * 10**8, moved=4 * 10**6,
    )
    kv_terms = exchange(kv_part, "mp")
    group = text_query.shape[1] // HD
    text_rows = text_kv.reshape(2 * rows, HD)
    wide = pltpu.VMEM((rows, group * HD), BF16)
    thin = pltpu.VMEM((2 * rows, HD), BF16)
    tall = shape((4 * rows, rows), F32)
    tall_slots = shape((16 * slots, HD))
    stats = call(
        text_kernel, tall, text_rows, text_query, out_cotangent,
        specs=[ANY] * 3, out_specs=ANY,
        scratch=[thin, wide, wide, pltpu.VMEM((3 * group, rows), F32), DMA((4,))], limit=WIDE,
        flops=10**9, moved=2 * 10**6,
    )
    kv_terms, stats = lax.optimization_barrier((kv_terms, stats))
    outgoing = call(
        pack_kernel, shape((2 * slots, HD)), kv_terms, code, specs=[VM, ANY],
        scratch=[pltpu.VMEM((8, HD), F32), DMA((1,))], flops=2 * 10**7, moved=10**6,
    )
    route = ("dp", "sec")
    incoming = exchange(outgoing.reshape(shards, 4, HD), route).reshape(2 * slots, HD)
    slot_rows = pltpu.VMEM(incoming.shape, BF16)
    grads, stats, kept = call(
        slots_kernel, (shape((2 * slots, HD)), tall, tall_slots),
        incoming, stats, text_query, out_cotangent, specs=[VM, ANY, ANY, ANY],
        out_specs=(VM, ANY, ANY), limit=SLOTL,
        scratch=[
            pltpu.VMEM((3 * group, rows), F32), wide, wide, pltpu.VMEM((2 * group, rows), F32),
            DMA((5,)),
        ],
        flops=10**9, moved=2 * 10**6,
    )
    returned = exchange(grads.reshape(shards, 4, HD), route).reshape(2 * slots, HD)
    attended = call(
        output_kernel, shape((rows, group * HD)), kept, text_rows, stats, text_query, specs=[ANY] * 4,
        scratch=[slot_rows, thin, pltpu.VMEM((2 * group, rows), F32), wide, DMA((4,))],
        limit=WIDE, flops=10**9, moved=2 * 10**6,
    )
    returned, attended = lax.optimization_barrier((returned, attended))
    row_grads = call(
        rows_kernel, shape((4, merged_rows, 2 * HD)), returned, code, flops=2 * 10**7, moved=5 * 10**5,
    )
    heads = exchange(row_grads, "mp")
    visual_grad = call(
        fold_kernel, shape((merged_rows, width)), heads, w_kv, flops=2 * 10**8, moved=3 * 10**6,
    )
    return (attended, visual_grad)


def solution(mesh):
    both = ("sec", "dp")
    in_specs = (
        P(both, "mp"), P(both), P(), P(None, None, "mp"), P("mp", None), P(), P(both), P(both),
        P("mp", None, None), P(both, "mp"), P(both, None, "mp"), P(both, "mp"),
    )
    return jax.shard_map(
        on_device, mesh=mesh, in_specs=in_specs, out_specs=(P(both, "mp"), P(both, "mp")),
        check_vma=False,
    )
```

```python
import math

import jax
import jax.numpy as jnp
from jax import lax
from jax.experimental import pallas as pl
from jax.experimental.pallas import tpu as pltpu
from jax.sharding import PartitionSpec as P

VIT_HD = 80
HD = 128
EPS = 1e-6
NEG = -1e30
EMPTY = 2.0**100
WIDE = 59
DP = 64
SLOTL = 53.5
LOG2E = math.log2(math.e)
SCALE2 = LOG2E / math.sqrt(HD)
F32 = jnp.float32
BF16 = jnp.bfloat16
VM = pl.BlockSpec(memory_space=pltpu.VMEM)
SM = pl.BlockSpec(memory_space=pltpu.SMEM)
ANY = pl.BlockSpec(memory_space=pl.ANY)
DMA = pltpu.SemaphoreType.DMA


def dot(a, b):
    return jnp.dot(a, b, preferred_element_type=F32)


def iota(shape, dim):
    return lax.broadcasted_iota(jnp.int32, shape, dim)


def call(kernel, out_shape, *args, flops=0, moved=0, limit=6, specs=None, out_specs=None, scratch=()):
    return pl.pallas_call(
        kernel,
        out_shape=out_shape,
        in_specs=specs or [VM] * len(args),
        out_specs=out_specs or jax.tree.map(lambda _: VM, out_shape),
        scratch_shapes=scratch,
        compiler_params=limit and pltpu.CompilerParams(vmem_limit_bytes=int(limit * 2**20)),
        cost_estimate=pl.CostEstimate(flops=flops, bytes_accessed=moved, transcendentals=0),
    )(*args)


def shape(dims, dtype=BF16):
    return jax.ShapeDtypeStruct(dims, dtype)


def one_hot(mask):
    return mask.astype(F32).astype(BF16)


def fetch(pairs, sems):
    copies = [pltpu.make_async_copy(a, b, sems.at[i]) for i, (a, b) in enumerate(pairs)]
    for copy in copies:
        copy.start()
    return copies


def code_kernel(rows_ref, dest_ref, code_ref):
    pieces = rows_ref.shape[1]
    a = iota((pieces, pieces), 0)
    b = iota((pieces, pieces), 1)
    rows = jnp.broadcast_to(rows_ref[...].astype(F32), (pieces, pieces))
    place = dest_ref[...]
    place = (place & (DP - 1)) * 2 + (place >> (DP.bit_length() - 1))
    dest = jnp.broadcast_to(place.astype(F32), (pieces, pieces))
    starts = jnp.sum(jnp.where(b < a, rows, 0.0), axis=1, keepdims=True)
    count = jnp.sum(jnp.where(b == a, rows, 0.0), axis=1, keepdims=True)
    target = jnp.sum(jnp.where(b == a, dest, 0.0), axis=1, keepdims=True)
    lane = iota((pieces, HD), 1)
    row = (lane & 63).astype(F32)
    inside = (row >= starts) & (row < starts + count)
    code = jnp.sum(jnp.where(inside, target * 4.0 + row - starts, 0.0), axis=0, keepdims=True)
    code_ref[...] = jnp.broadcast_to(code, (8, HD)) + 2.0 * (iota((8, HD), 1) >> 6).astype(F32)


def vit_kernel(
    pos_ref, gain_hbm, win_hbm, wt_hbm, x_hbm, proj_hbm, part_ref, own_ref,
    gain_ref, win_ref, wt_ref, x_ref, proj_ref, w_ref, sems,
):
    pairs = [(gain_hbm, gain_ref), (x_hbm, x_ref), (wt_hbm, wt_ref)]
    pairs += [(win_hbm, win_ref), (proj_hbm, proj_ref)]
    copies = fetch(pairs, sems)
    width, points = x_ref.shape
    copies[0].wait()
    copies[1].wait()
    x = x_ref[...]
    local = proj_ref.shape[0]
    xf = x.astype(F32)
    scale = lax.rsqrt(jnp.sum(xf * xf, axis=0, keepdims=True) * (1.0 / width) + EPS)
    copies[2].wait()
    for i in range(width // HD):
        cols = slice(i * HD, (i + 1) * HD)
        w_ref[:, cols] = (wt_ref[:, cols].astype(F32) * gain_ref[i : i + 1].astype(F32)).astype(BF16)
    qkv = (dot(w_ref[...], x) * scale).astype(BF16)
    copies[3].wait()
    wins = jnp.broadcast_to(win_ref[...].astype(F32), (8, points))
    bias = jnp.where(wins.T[:, :1] == wins[:1], 0.0, NEG)
    mixed = []
    for h in range(local // VIT_HD):
        q = qkv[h * VIT_HD : (h + 1) * VIT_HD]
        k = qkv[local + h * VIT_HD : local + (h + 1) * VIT_HD]
        v = qkv[2 * local + h * VIT_HD : 2 * local + (h + 1) * VIT_HD]
        s = dot(k.T, q) * (LOG2E / math.sqrt(VIT_HD)) + bias
        e = jnp.exp2(s - jnp.max(s, axis=0, keepdims=True))
        weights = (e * (1.0 / jnp.sum(e, axis=0, keepdims=True))).astype(BF16)
        mixed.append(dot(v, weights).astype(BF16))
    mixed = jnp.concatenate(mixed, axis=0)
    n = iota((points, points), 1)
    perm = one_hot(iota((points, points), 0) == 4 * (n & 63) + (n >> 6))
    mixed = dot(mixed, perm).astype(BF16)
    copies[4].wait()
    part = dot(mixed.T, proj_ref[...]).astype(BF16)
    for m in range(4):
        part_ref[m] = part[m * 64 : (m + 1) * 64]
    sel = one_hot(iota((points, 64), 0) == 4 * iota((points, 64), 1) + pos_ref[0])
    own_ref[...] = dot(x, sel).astype(BF16).T


def merge_kernel(in_ref, own_ref, gain_ref, w_ref, out_ref):
    resid = own_ref[...].astype(F32)
    for m in range(4):
        resid = resid + in_ref[m].astype(F32)
    scale = lax.rsqrt(jnp.mean(resid * resid, axis=1, keepdims=True) + EPS)
    merged = (resid * scale * gain_ref[...].astype(F32)).astype(BF16)
    kv = dot(merged, w_ref[...]).astype(BF16)
    for h in range(4):
        out_ref[h] = kv[:, h * 256 : (h + 1) * 256]


def pack_kernel(in_ref, code_hbm, out_ref, code_ref, sems):
    copies = fetch([(code_hbm, code_ref)], sems)
    kv = in_ref[0].astype(F32)
    for m in range(1, 4):
        kv = kv + in_ref[m].astype(F32)
    kv = kv.astype(BF16)
    stack = jnp.concatenate([kv[:, :HD], kv[:, HD:]], axis=0)
    copies[0].wait()
    dims = out_ref.shape
    row = iota(dims, 0)
    picks = one_hot(row.astype(F32) == code_ref[:1])
    filled = dot(picks, jnp.ones((HD, HD), BF16))
    empty = jnp.where(((row & 2) == 0) & (filled < 0.5), EMPTY, 0.0)
    out_ref[...] = (dot(picks, stack) + empty).astype(BF16)


def head_of(tall, ref):
    return tall.at[pl.ds(0, ref.shape[0])]


def text_kernel(kv_hbm, q_hbm, c_hbm, stats_hbm, kv_ref, q_ref, c_ref, stats_ref, sems):
    head = fetch([(kv_hbm, kv_ref)], sems.at[pl.ds(0, 1)])[0]
    copies = fetch([(q_hbm, q_ref), (c_hbm, c_ref)], sems.at[pl.ds(1, 2)])
    group = q_ref.shape[1] // HD
    rows = q_ref.shape[0]
    head.wait()
    k, v = text_pair(kv_ref)
    causal = iota((rows, rows), 0) <= iota((rows, rows), 1)
    for g in range(group):
        if g == 0:
            for copy in copies:
                copy.wait()
        s = jnp.where(causal, dot(k, q_ref[:, g * HD : (g + 1) * HD].T) * SCALE2, NEG)
        m = jnp.max(s, axis=0, keepdims=True)
        e = jnp.exp2(s - m)
        dp = dot(v, c_ref[:, g * HD : (g + 1) * HD].T)
        stats_ref[g : g + 1] = m
        stats_ref[group + g : group + g + 1] = jnp.sum(e, axis=0, keepdims=True)
        stats_ref[2 * group + g : 2 * group + g + 1] = jnp.sum(e * dp, axis=0, keepdims=True)
    fetch([(stats_ref, head_of(stats_hbm, stats_ref))], sems.at[pl.ds(3, 1)])[0].wait()


def text_pair(kv_ref):
    a = iota((HD, HD), 0)
    order = one_hot(iota((HD, HD), 1) == 2 * (a & 63) + (a >> 6))
    return split(order, kv_ref)


def split(order, ref):
    keys = []
    values = []
    for b in range(ref.shape[0] // HD):
        part = dot(order, ref[b * HD : (b + 1) * HD]).astype(BF16)
        keys.append(part[:64])
        values.append(part[64:])
    return jnp.concatenate(keys, axis=0), jnp.concatenate(values, axis=0)


def slot_place(j):
    return 4 * ((j & 63) >> 1) + 2 * (j >> 6) + (j & 1)


def slot_pair(in_ref):
    order = one_hot(iota((HD, HD), 1) == slot_place(iota((HD, HD), 0)))
    keys, values = split(order, in_ref)
    live = jnp.broadcast_to(keys[:, :1].astype(F32) < 0.5 * EMPTY, keys.shape)
    bias = jnp.where(live, 0.0, NEG)
    keys = jnp.where(live, keys.astype(F32), 0.0).astype(BF16)
    return keys, values, jnp.concatenate([bias, bias], axis=1)


def slots_kernel(
    in_ref, text_hbm, q_hbm, c_hbm, out_ref, stats_hbm, in_hbm,
    text_ref, q_ref, c_ref, stats_ref, sems,
):
    copies = fetch([(q_hbm, q_ref), (c_hbm, c_ref)], sems.at[pl.ds(1, 2)])
    pairs = [(head_of(text_hbm, text_ref), text_ref)]
    stats = fetch(pairs, sems.at[pl.ds(0, 1)])[0]
    kept = fetch([(in_ref, head_of(in_hbm, in_ref))], sems.at[pl.ds(4, 1)])[0]
    group = q_ref.shape[1] // HD
    k, v, bias = slot_pair(in_ref)
    slots = k.shape[0]
    stats.wait()
    dk = jnp.zeros((slots, HD), F32)
    dv = jnp.zeros((slots, HD), F32)
    held = [[], [], [], []]
    for g in range(group):
        if g == 0:
            for copy in copies:
                copy.wait()
        q = q_ref[:, g * HD : (g + 1) * HD]
        c = c_ref[:, g * HD : (g + 1) * HD]
        s = dot(k, q.T) * SCALE2 + bias
        dp = dot(v, c.T)
        mt = text_ref[g : g + 1]
        m = jnp.maximum(mt, jnp.max(s, axis=0, keepdims=True))
        e = jnp.exp2(s - m)
        alpha = jnp.exp2(mt - m)
        total = text_ref[group + g : group + g + 1] * alpha + jnp.sum(e, axis=0, keepdims=True)
        inv = 1.0 / total
        delta = text_ref[2 * group + g : 2 * group + g + 1] * alpha
        delta = (delta + jnp.sum(e * dp, axis=0, keepdims=True)) * inv
        stats_ref[g : g + 1] = m
        stats_ref[group + g : group + g + 1] = inv
        p = e * inv
        lists = ((p * (dp - delta)).astype(BF16), p.astype(BF16), q, c)
        for some, one in zip(held, lists):
            some.append(one)
        if g % (group // 2) == group // 2 - 1:
            ds, ps = (jnp.concatenate(some, axis=1) for some in held[:2])
            qs, cs = (jnp.concatenate(some, axis=0) for some in held[2:])
            dk = dk + dot(ds, qs)
            dv = dv + dot(ps, cs)
            held = [[], [], [], []]
    sent = fetch([(stats_ref, head_of(stats_hbm, stats_ref))], sems.at[pl.ds(3, 1)])[0]
    dk = (dk * (1.0 / math.sqrt(HD))).astype(BF16)
    dv = dv.astype(BF16)
    order = one_hot(iota((HD, HD), 0) == slot_place(iota((HD, HD), 1)))
    for b in range(slots // 64):
        pair = jnp.concatenate([dk[b * 64 : (b + 1) * 64], dv[b * 64 : (b + 1) * 64]], axis=0)
        out_ref[b * HD : (b + 1) * HD] = dot(order, pair).astype(BF16)
    sent.wait()
    kept.wait()


def output_kernel(
    in_hbm, kv_hbm, stats_hbm, q_hbm, out_ref, in_ref, kv_ref, stats_ref, q_ref, sems
):
    pairs = [(kv_hbm, kv_ref), (head_of(in_hbm, in_ref), in_ref), (q_hbm, q_ref)]
    pairs += [(head_of(stats_hbm, stats_ref), stats_ref)]
    copies = fetch(pairs, sems)
    group = q_ref.shape[1] // HD
    rows = q_ref.shape[0]
    copies[0].wait()
    kt, vt = text_pair(kv_ref)
    copies[1].wait()
    ks, vs, bias = slot_pair(in_ref)
    copies[2].wait()
    copies[3].wait()
    values = jnp.concatenate([vt, vs], axis=0).T
    causal = iota((rows, rows), 0) <= iota((rows, rows), 1)
    for g in range(group):
        qt = q_ref[:, g * HD : (g + 1) * HD].T
        m = stats_ref[g : g + 1]
        inv = stats_ref[group + g : group + g + 1]
        text = jnp.where(causal, dot(kt, qt) * SCALE2, NEG)
        slot = dot(ks, qt) * SCALE2 + bias
        s = jnp.concatenate([text, slot], axis=0)
        o = dot(values, (jnp.exp2(s - m) * inv).astype(BF16))
        out_ref[:, g * HD : (g + 1) * HD] = o.T.astype(BF16)


def rows_kernel(in_ref, code_ref, out_ref):
    code = jnp.broadcast_to(code_ref[:1], (HD, HD)).T
    count = in_ref.shape[0]
    picks = one_hot(iota((HD, count), 1).astype(F32) == code[:, :1])
    g = dot(picks, in_ref[...]).astype(BF16)
    half = HD // 2
    for m in range(4):
        out_ref[m, :, :HD] = g[:half]
        out_ref[m, :, HD:] = g[half:]


def fold_kernel(in_ref, w_ref, out_ref):
    grads = jnp.concatenate([in_ref[h] for h in range(4)], axis=1)
    out_ref[...] = dot(w_ref[...], grads.T).T.astype(BF16)


def exchange(x, axes):
    return lax.all_to_all(x, axes, split_axis=0, concat_axis=0, tiled=True)


def on_device(
    patches, window_index, vit_gain, vit_qkv, vit_proj, merge_gain, piece_rows, piece_dest,
    visual_kv, text_query, text_kv, out_cotangent,
):
    shards = lax.axis_size("sec") * lax.axis_size("dp")
    position = lax.axis_index("mp").astype(jnp.int32).reshape(1)
    points, width_part = patches.shape
    width = vit_qkv.shape[0]
    local = vit_qkv.shape[2]
    rows = text_query.shape[0]
    slots = 2 * shards
    merged_rows = points // 4

    x = lax.all_gather(patches.T, "mp", axis=0, tiled=True)
    wt = jnp.transpose(vit_qkv, (1, 2, 0)).reshape(3 * local, width)
    part, own = call(
        vit_kernel, (shape((4, merged_rows, width)), shape((merged_rows, width))),
        position, vit_gain.reshape(-1, HD), window_index.reshape(1, points), wt, x, vit_proj,
        specs=[SM] + [ANY] * 5, limit=WIDE, flops=10**9, moved=4 * 10**6,
        scratch=[
            pltpu.VMEM((width // HD, HD), BF16), pltpu.VMEM((1, points), jnp.int32),
            pltpu.VMEM((3 * local, width), BF16), pltpu.VMEM((width, points), BF16),
            pltpu.VMEM((local, width), BF16), pltpu.VMEM((3 * local, width), BF16), DMA((5,)),
        ],
    )
    code = call(
        code_kernel, shape((8, HD), F32), piece_rows.reshape(1, -1), piece_dest.reshape(1, -1),
        flops=10**6, moved=10**4,
    )
    summed = exchange(part, "mp")
    w_kv = jnp.transpose(visual_kv.reshape(width, 2, 4, HD), (0, 2, 1, 3)).reshape(width, 8 * HD)
    kv_part = call(
        merge_kernel, shape((4, merged_rows, 2 * HD)),
        summed, own, merge_gain.reshape(1, width), w_kv, flops=2 * 10**8, moved=4 * 10**6,
    )
    kv_terms = exchange(kv_part, "mp")
    group = text_query.shape[1] // HD
    text_rows = text_kv.reshape(2 * rows, HD)
    wide = pltpu.VMEM((rows, group * HD), BF16)
    thin = pltpu.VMEM((2 * rows, HD), BF16)
    tall = shape((4 * rows, rows), F32)
    tall_slots = shape((16 * slots, HD))
    stats = call(
        text_kernel, tall, text_rows, text_query, out_cotangent,
        specs=[ANY] * 3, out_specs=ANY,
        scratch=[thin, wide, wide, pltpu.VMEM((3 * group, rows), F32), DMA((4,))], limit=WIDE,
        flops=10**9, moved=2 * 10**6,
    )
    kv_terms, stats = lax.optimization_barrier((kv_terms, stats))
    outgoing = call(
        pack_kernel, shape((2 * slots, HD)), kv_terms, code, specs=[VM, ANY],
        scratch=[pltpu.VMEM((8, HD), F32), DMA((1,))], flops=2 * 10**7, moved=10**6,
    )
    route = ("dp", "sec")
    incoming = exchange(outgoing.reshape(shards, 4, HD), route).reshape(2 * slots, HD)
    slot_rows = pltpu.VMEM(incoming.shape, BF16)
    grads, stats, kept = call(
        slots_kernel, (shape((2 * slots, HD)), tall, tall_slots),
        incoming, stats, text_query, out_cotangent, specs=[VM, ANY, ANY, ANY],
        out_specs=(VM, ANY, ANY), limit=SLOTL,
        scratch=[
            pltpu.VMEM((3 * group, rows), F32), wide, wide, pltpu.VMEM((2 * group, rows), F32),
            DMA((5,)),
        ],
        flops=10**9, moved=2 * 10**6,
    )
    returned = exchange(grads.reshape(shards, 4, HD), route).reshape(2 * slots, HD)
    attended = call(
        output_kernel, shape((rows, group * HD)), kept, text_rows, stats, text_query, specs=[ANY] * 4,
        scratch=[slot_rows, thin, pltpu.VMEM((2 * group, rows), F32), wide, DMA((4,))],
        limit=WIDE, flops=10**9, moved=2 * 10**6,
    )
    returned, attended = lax.optimization_barrier((returned, attended))
    row_grads = call(
        rows_kernel, shape((4, merged_rows, 2 * HD)), returned, code, flops=2 * 10**7, moved=5 * 10**5,
    )
    heads = exchange(row_grads, "mp")
    visual_grad = call(
        fold_kernel, shape((merged_rows, width)), heads, w_kv, flops=2 * 10**8, moved=3 * 10**6,
    )
    return (attended, visual_grad)


def solution(mesh):
    both = ("sec", "dp")
    in_specs = (
        P(both, "mp"), P(both), P(), P(None, None, "mp"), P("mp", None), P(), P(both), P(both),
        P("mp", None, None), P(both, "mp"), P(both, None, "mp"), P(both, "mp"),
    )
    return jax.shard_map(
        on_device, mesh=mesh, in_specs=in_specs, out_specs=(P(both, "mp"), P(both, "mp")),
        check_vma=False,
    )
```
